512 devices in a mesh: site: 16 (over z, core), dev: 32 (over y, x).
Axes of the slice: x: 4, y: 8, z: 8, core: 2. Of those that a mesh axis runs over, the one named last changes fastest.
Arguments:
- tokens: bfloat16 [16, 4096, 8192], P('site', 'dev'), may hold values from -6 to 6
- cotangent: bfloat16 [16, 4096, 256], P('site', 'dev'), may hold values from -0.119628906 to 0.119628906
- weight: bfloat16 [256, 8192], P('dev'), may hold values from -0.0625 to 0.0625
- momentum: float32 [16, 256, 8192], P('site', 'dev'), may hold values from -6 to 6
- kept_index: int32 [16, 256, 128, 16], P(None, 'dev'), may hold values from 0 to 63, all different within a row
Outputs:
- scores: bfloat16 [16, 4096, 256], P('site', 'dev')
- momentum_out: float32 [16, 256, 8192], P('site', 'dev')
The draws below stay inside these ranges and needn't reach their ends.
Inputs may be any that keep to these rules, and one draw needn't show every extreme that they name: `kept_index`: the 16 indices of one block and site are all different.
All inputs are finite; a program needn't handle non-finite values.
Results may differ from the reference program's by a relative error of at most 0.022.
Values may be sent and summed in bfloat16 or wider, within the bound.
No kernel may reach another device: no remote copies, remote signals or barrier semaphores. Data moves between devices by JAX's collectives and lax.ppermute only.
A program may use at most 64 MiB of HBM per device.

```python
import jax
import jax.numpy as jnp
from jax import lax

C = 8192
SPAN = 64
K = 16
TOK_DEV = 128
SITES = 16
ROWS = 256
TOKENS = 4096
BLOCKS = 128
N_DEV = 32


def steps_of(own_key, dims, split, least, top_value):
    factor_of = 1.0
    for position, blocks in split:
        draws = jax.random.uniform(jax.random.fold_in(jax.random.fold_in(own_key, 6), position), (blocks,), jnp.float32, least / len(split), top_value / len(split))
        factor_of = factor_of * jnp.repeat(jnp.exp(draws), dims[position] // blocks).reshape((-1,) + (1,) * (len(dims) - 1 - position))
    return factor_of


def picks_of(rng, rows, amount, top, lift):
    sequence = jax.random.permutation(jax.random.fold_in(rng, 1), amount)
    pull = sequence
    for power in range(3):
        pull = pull * pull // amount
    pull = pull * lift // amount
    lots = jax.random.randint(jax.random.fold_in(rng, 2), (rows, amount), 0, 4096) + pull
    holders = jax.random.permutation(jax.random.fold_in(rng, 3), rows)[jnp.arange(amount) % rows]
    lots = jnp.where(jnp.arange(rows)[:, None] == holders[None, :], 1 << 14, lots)
    score = lots * amount + jnp.arange(amount)
    return lax.top_k(score.astype(jnp.int32), top)[1].astype(jnp.int32)


def bell_draw(own_key, dims, width, bound, shards=(), held_as=jnp.bfloat16):
    entries = width * jax.random.normal(own_key, dims, jnp.float32)
    if shards:
        entries = entries * steps_of(own_key, dims, shards, -0.22, 0.18)
    return jnp.clip(entries, -bound, bound).astype(held_as)


def setup_inputs(seed: int = 0) -> dict:
    seeds = jax.random.split(jax.random.key(seed), 6)
    tokens = bell_draw(seeds[0], (SITES, TOKENS, C), 1.0, 6.0, ((0, 16), (1, 32)))
    cotangent = bell_draw(seeds[1], (SITES, TOKENS, ROWS), 0.02, 0.119628906, ((0, 16), (1, 32)))
    weight = bell_draw(seeds[2], (ROWS, C), C ** -0.5, 0.0625, ((0, 32),))
    momentum = bell_draw(seeds[3], (SITES, ROWS, C), 1.0, 6.0, ((0, 16), (1, 32)), jnp.float32)
    kept_index = picks_of(seeds[4], SITES * ROWS * BLOCKS, SPAN, K, 0).reshape((SITES, ROWS, BLOCKS, K))
    return {"tokens": tokens, "cotangent": cotangent, "weight": weight, "momentum": momentum, "kept_index": kept_index}


momentum_decay = 0.999
step_size = 0.01

def dct_table():
    freq = jnp.arange(64)[:, None].astype(jnp.float32)
    place = jnp.arange(64)[None, :].astype(jnp.float32)
    factor = jnp.where(freq == 0.0, jnp.sqrt(1.0 / 64.0), jnp.sqrt(2.0 / 64.0)).astype(jnp.float32)
    return (factor * jnp.cos(jnp.pi * (2.0 * place + 1.0) * freq / 128.0)).astype(jnp.float32)

def forward_dct(field, table):
    blocks = field.reshape(field.shape[0], -1, 64)
    return jnp.einsum('rcn,kn->rck', blocks, table, precision=lax.Precision.HIGHEST)

def inverse_dct(coefs, table):
    blocks = jnp.einsum('rck,kn->rcn', coefs, table, precision=lax.Precision.HIGHEST)
    return blocks.reshape(coefs.shape[0], -1)

def reference(tokens, cotangent, weight, momentum, kept_index):
    table = dct_table()
    iota_block = jnp.arange(64).astype(jnp.int32)

    def site_step(running, inputs):
        site_tokens, site_cotan, site_moment, site_index = inputs
        token_groups = site_tokens.reshape(N_DEV, TOK_DEV, C)
        cotan_groups = site_cotan.reshape(N_DEV, TOK_DEV, ROWS)

        def add_term(group, accum):
            term = lax.dot_general(cotan_groups[group], token_groups[group], (((0,), (0,)), ((), ())), preferred_element_type=jnp.float32)
            rounded = lax.optimization_barrier(term.astype(jnp.bfloat16))
            return accum + rounded.astype(jnp.float32)
        grad = lax.fori_loop(0, N_DEV, add_term, jnp.zeros((ROWS, C), jnp.float32))
        raised = momentum_decay * site_moment + grad
        coefs = forward_dct(raised, table)
        keep_mask = jnp.any(site_index[..., None] == iota_block, axis=2).astype(jnp.float32)
        picked = coefs * keep_mask
        moment_new = raised - inverse_dct(picked, table)
        sent = lax.optimization_barrier(picked.astype(jnp.bfloat16))
        return (running + sent.astype(jnp.float32), moment_new)
    zero_total = jnp.zeros((ROWS, C // 64, 64), jnp.float32)
    total, momentum_out = lax.scan(site_step, zero_total, (tokens, cotangent, momentum, kept_index))
    decoded = inverse_dct(total, table)
    new_weight = (weight.astype(jnp.float32) - step_size * decoded).astype(jnp.bfloat16)

    def project(site_tokens):
        return lax.dot_general(site_tokens, new_weight, (((1,), (1,)), ((), ())), preferred_element_type=jnp.float32).astype(jnp.bfloat16)
    scores = lax.map(project, tokens)
    return (scores, momentum_out)
```

```python
import numpy as np
import jax
import jax.numpy as jnp
from jax import lax
from jax.sharding import Mesh, PartitionSpec as P

momentum_decay = 0.999
step_size = 0.01
SITE = ("z", "core")
DEV = ("y", "x")


def pair_table():
    freq = np.arange(64)[:, None]
    place = np.arange(64)[None, :]
    factor = np.where(freq == 0, np.sqrt(1.0 / 64.0), np.sqrt(2.0 / 64.0))
    one = factor * np.cos(np.pi * (2.0 * place + 1.0) * freq / 128.0)
    return np.kron(np.eye(2), one).astype(np.float32)


def exact_dot(a, b):
    return jnp.dot(a, b, precision=lax.Precision.HIGHEST)


def shards(tokens, cotangent, weight, momentum, kept_index):
    nz, ncore, ny, nx = (lax.axis_size(name) for name in ("z", "core", "y", "x"))
    site = lax.axis_index(SITE)
    sites = nz * ncore
    _, tok, width = tokens.shape
    rows_all = cotangent.shape[2]
    rows = weight.shape[0]
    part = width // nx
    tiles = width // 128
    table = pair_table()

    sliced = tokens[0].reshape(tok, nx, part).transpose(1, 0, 2)
    cotans = jnp.broadcast_to(cotangent, (nx, tok, rows_all))
    joined = lax.all_to_all(jnp.concatenate([sliced, cotans], axis=2), "x", 0, 0, tiled=True)
    tok_x = joined[:, :, :part].reshape(nx * tok, part)
    cot_x = joined[:, :, part:].reshape(nx * tok, rows_all)

    own = lax.dynamic_index_in_dim(kept_index, site, 0, keepdims=False)
    own = own.reshape(rows, tiles, 2, -1) + jnp.array([0, 64], jnp.int32)[None, None, :, None]
    own = own.reshape(rows, tiles, -1).transpose(1, 0, 2)
    keep = jnp.any(own[..., None] == jnp.arange(128, dtype=jnp.int32), axis=2)
    keep = keep.astype(jnp.float32).reshape(tiles * rows, 128)

    partial = lax.dot_general(
        cot_x, tok_x, (((0,), (0,)), ((), ())), preferred_element_type=jnp.float32
    ).astype(jnp.bfloat16)
    terms = lax.all_to_all(partial.reshape(ny * nx, rows, part), DEV, 0, 0, tiled=True)
    grad = jnp.sum(terms.reshape(ny, nx, rows, part).astype(jnp.float32), axis=0)
    grad = grad.reshape(nx, rows, part // 128, 128).transpose(0, 2, 1, 3).reshape(tiles * rows, 128)
    moment = momentum[0].reshape(rows, tiles, 128).transpose(1, 0, 2).reshape(tiles * rows, 128)
    raised = momentum_decay * moment + grad
    picked = exact_dot(raised, table.T) * keep
    moment_new = raised - exact_dot(picked, table)
    moment_new = moment_new.reshape(tiles, rows, 128).transpose(1, 0, 2).reshape(1, rows, width)

    sent = picked.astype(jnp.bfloat16).reshape(nx, sites, rows, 128).transpose(1, 0, 2, 3)
    sent = lax.all_to_all(sent, SITE, 0, 0, tiled=True)
    total = jnp.sum(sent.astype(jnp.float32), axis=0).reshape(nx * rows, 128)
    decoded = exact_dot(total, table).reshape(nx, rows, 128)
    held = weight.reshape(rows, nx, sites, 128).transpose(2, 1, 0, 3)
    held = lax.dynamic_index_in_dim(held, site, 0, keepdims=False)
    fresh = (held.astype(jnp.float32) - step_size * decoded).astype(jnp.bfloat16)

    spread = jnp.broadcast_to(fresh[None], (nz, nx, rows, 128)).reshape(nz * nx, rows, 128)
    got = lax.all_to_all(spread, ("z", "x"), 0, 0, tiled=True)
    got = got.reshape(nz, nx * rows, 128).transpose(1, 0, 2).reshape(1, nx * rows, nz * 128)
    got = lax.all_to_all(jnp.broadcast_to(got, (ny, nx * rows, nz * 128)), "y", 0, 0, tiled=True)
    mine = got.reshape(rows_all, nz * 128)
    other = lax.ppermute(mine, "core", [(0, 1), (1, 0)])
    core = lax.axis_index("core")
    tok_pairs = tok_x.reshape(nx * tok, nz, ncore, 128)
    tok_mine = lax.dynamic_index_in_dim(tok_pairs, core, 2, keepdims=False).reshape(nx * tok, nz * 128)
    tok_other = lax.dynamic_index_in_dim(tok_pairs, 1 - core, 2, keepdims=False).reshape(nx * tok, nz * 128)
    across = (((1,), (1,)), ((), ()))
    scores = lax.dot_general(tok_mine, mine, across, preferred_element_type=jnp.float32)
    scores = scores + lax.dot_general(tok_other, other, across, preferred_element_type=jnp.float32)
    scores = lax.all_to_all(scores.reshape(nx, tok, rows_all), "x", 0, 0, tiled=True)
    scores = jnp.sum(scores, axis=0).astype(jnp.bfloat16)
    return (scores[None], moment_new)


def solution(mesh):
    grid = Mesh(mesh.devices.reshape(8, 2, 8, 4), ("z", "core", "y", "x"))
    placed = (
        P(SITE, DEV, None),
        P(SITE, DEV, None),
        P(DEV, None),
        P(SITE, DEV, None),
        P(None, DEV, None, None),
    )
    return jax.shard_map(
        shards,
        mesh=grid,
        in_specs=placed,
        out_specs=(P(SITE, DEV, None), P(SITE, DEV, None)),
        check_vma=False,
    )
```

```python
import numpy as np
import jax
import jax.numpy as jnp
from jax import lax
from jax.experimental import pallas as pl
from jax.experimental.pallas import tpu as pltpu
from jax.sharding import Mesh, PartitionSpec as P

momentum_decay = 0.999
step_size = 0.01
SITE = ("z", "core")
GROUP = ("yl", "x")
DEV = ("yh", "yl", "x")
VMEM_LIMIT = 48 * 1024 * 1024


def pair_table():
    freq = np.arange(64)[:, None]
    place = np.arange(64)[None, :]
    factor = np.where(freq == 0, np.sqrt(1.0 / 64.0), np.sqrt(2.0 / 64.0))
    one = factor * np.cos(np.pi * (2.0 * place + 1.0) * freq / 128.0)
    return np.kron(np.eye(2), one).astype(np.float32)


def exact_dot(a, b):
    return jnp.dot(a, b, precision=lax.Precision.HIGHEST, preferred_element_type=jnp.float32)


def params():
    return pltpu.CompilerParams(vmem_limit_bytes=VMEM_LIMIT)


def pack(tokens, cotangent, groups):
    tok, width = tokens.shape
    part = width // groups
    rows_all = cotangent.shape[1]
    fold = part // rows_all
    extra = tok // fold

    def body(tok_ref, cot_ref, out_ref):
        out_ref[0, :tok, :] = tok_ref[...]
        for q in range(fold):
            out_ref[0, tok:, q * rows_all:(q + 1) * rows_all] = cot_ref[q * extra:(q + 1) * extra, :]

    return pl.pallas_call(
        body,
        grid=(groups,),
        in_specs=[
            pl.BlockSpec((tok, part), lambda g: (0, g)),
            pl.BlockSpec((tok, rows_all), lambda g: (0, 0)),
        ],
        out_specs=pl.BlockSpec((1, tok + extra, part), lambda g: (g, 0, 0)),
        out_shape=jax.ShapeDtypeStruct((groups, tok + extra, part), tokens.dtype),
        compiler_params=params(),
        name="pack",
    )(tokens, cotangent)


def gradient(joined, tok, rows_all):
    groups, high, part = joined.shape
    extra = high - tok
    fold = tok // extra
    cols = 256

    def body(tok_ref, cot_ref, out_ref):
        left = jnp.concatenate(
            [
                cot_ref[k, :, q * rows_all:(q + 1) * rows_all]
                for k in range(groups)
                for q in range(fold)
            ],
            axis=0,
        )
        right = tok_ref[...].reshape(groups * tok, cols)
        out_ref[...] = lax.dot_general(
            left, right, (((0,), (0,)), ((), ())), preferred_element_type=jnp.float32
        ).astype(out_ref.dtype)

    return pl.pallas_call(
        body,
        grid=(part // cols,),
        in_specs=[
            pl.BlockSpec((groups, tok, cols), lambda j: (0, 0, j)),
            pl.BlockSpec((groups, extra, part), lambda j: (0, tok // extra, 0)),
        ],
        out_specs=pl.BlockSpec((rows_all, cols), lambda j: (0, j)),
        out_shape=jax.ShapeDtypeStruct((rows_all, part), jnp.bfloat16),
        compiler_params=params(),
        name="gradient",
    )(joined, joined)


def raise_and_pick(terms, momentum, keep, table, groups, nz, ncore):
    rows, width = momentum.shape
    part = width // groups
    tiles = part // 128

    def body(terms_ref, mom_ref, keep_ref, table_ref, out_ref, sent_ref):
        pieces = []
        for g in range(groups):
            grad = terms_ref[g].astype(jnp.float32)
            for k in range(g + groups, terms_ref.shape[0], groups):
                grad = grad + terms_ref[k].astype(jnp.float32)
            raised = momentum_decay * mom_ref[:, g * part:(g + 1) * part] + grad
            pieces += [raised[:, t * 128:(t + 1) * 128] for t in range(tiles)]
        raised = jnp.concatenate(pieces, axis=0)
        both = table_ref[...]
        picked = exact_dot(raised, both.T) * keep_ref[...]
        moment_new = raised - exact_dot(picked, both)
        sent = picked.astype(jnp.bfloat16)
        for g in range(groups):
            for t in range(tiles):
                at = (g * tiles + t) * rows
                out_ref[:, g * part + t * 128:g * part + (t + 1) * 128] = moment_new[at:at + rows]
                for c in range(ncore):
                    sent_ref[t * ncore + c, g] = sent[at:at + rows]

    return pl.pallas_call(
        body,
        out_shape=(
            jax.ShapeDtypeStruct((rows, width), jnp.float32),
            jax.ShapeDtypeStruct((nz * ncore, groups, rows, 128), jnp.bfloat16),
        ),
        compiler_params=params(),
        name="raise_and_pick",
    )(terms, momentum, keep, table)


def update(sent, held, table, copies):
    sites, groups, rows, lanes = sent.shape

    def body(sent_ref, held_ref, table_ref, out_ref):
        total = sent_ref[0].astype(jnp.float32)
        for s in range(1, sites):
            total = total + sent_ref[s].astype(jnp.float32)
        decoded = exact_dot(total.reshape(groups * rows, lanes), table_ref[...])
        fresh = held_ref[...].astype(jnp.float32) - step_size * decoded.reshape(groups, rows, lanes)
        fresh = fresh.astype(jnp.bfloat16)
        for c in range(copies):
            out_ref[c] = fresh

    return pl.pallas_call(
        body,
        out_shape=jax.ShapeDtypeStruct((copies, groups, rows, lanes), jnp.bfloat16),
        compiler_params=params(),
        name="update",
    )(sent, held, table)


def project(joined, fresh, tok):
    groups, _, part = joined.shape
    tiles, rows_all, _ = fresh.shape

    def body(tok_ref, fresh_ref, out_ref):
        weight = jnp.concatenate([fresh_ref[t] for t in range(tiles)], axis=1)
        out_ref[0] = lax.dot_general(
            tok_ref[0], weight, (((1,), (1,)), ((), ())), preferred_element_type=jnp.float32
        ).astype(out_ref.dtype)

    return pl.pallas_call(
        body,
        grid=(groups,),
        in_specs=[
            pl.BlockSpec((1, tok, part), lambda g: (g, 0, 0)),
            pl.BlockSpec((tiles, rows_all, 128), lambda g: (0, 0, 0)),
        ],
        out_specs=pl.BlockSpec((1, tok, rows_all), lambda g: (g, 0, 0)),
        out_shape=jax.ShapeDtypeStruct((groups, tok, rows_all), jnp.bfloat16),
        compiler_params=params(),
        name="project",
    )(joined, fresh)


def exchange(value, axes):
    return lax.all_to_all(value, axes, 0, 0, tiled=True)


def shards(tokens, cotangent, weight, momentum, kept_index):
    nz, ncore, nyh, nyl, nx = (lax.axis_size(name) for name in ("z", "core", "yh", "yl", "x"))
    groups = nyl * nx
    site = lax.axis_index(SITE)
    _, tok, width = tokens.shape
    rows_all = cotangent.shape[2]
    rows = weight.shape[0]
    part = width // groups
    table = jnp.asarray(pair_table())

    joined = exchange(pack(tokens[0], cotangent[0], groups), GROUP)

    tiles = width // 128
    own = lax.dynamic_index_in_dim(kept_index, site, 0, keepdims=False)
    own = own.reshape(rows, tiles, 2, -1) + jnp.array([0, 64], jnp.int32)[None, None, :, None]
    own = own.reshape(rows, tiles, -1).transpose(1, 0, 2)
    keep = jnp.any(own[..., None] == jnp.arange(128, dtype=jnp.int32), axis=2)
    keep = keep.astype(jnp.float32).reshape(tiles * rows, 128)
    held = weight.reshape(rows, groups, part // 128, 128)
    held = lax.dynamic_index_in_dim(held, lax.axis_index("z"), 2, keepdims=False).transpose(1, 0, 2)

    partial = gradient(joined, tok, rows_all)
    terms = exchange(partial.reshape(nyh * groups, rows, part), DEV)
    moment_new, sent = raise_and_pick(terms, momentum[0], keep, table, groups, nz, ncore)

    fresh = update(exchange(sent, SITE), held, table, nz * nyh)
    fresh = exchange(fresh.reshape(nz * nyh * groups, rows, 128), ("z",) + DEV)
    scores = project(joined, fresh.reshape(nz, rows_all, 128), tok)
    scores = exchange(scores, GROUP)
    scores = jnp.sum(scores.astype(jnp.float32), axis=0).astype(jnp.bfloat16)
    return (scores[None], moment_new[None])


def solution(mesh):
    grid = Mesh(mesh.devices.reshape(8, 2, 4, 2, 4), ("z", "core", "yh", "yl", "x"))
    placed = (
        P(SITE, DEV, None),
        P(SITE, DEV, None),
        P(DEV, None),
        P(SITE, DEV, None),
        P(None, DEV, None, None),
    )
    return jax.shard_map(
        shards,
        mesh=grid,
        in_specs=placed,
        out_specs=(P(SITE, DEV, None), P(SITE, DEV, None)),
        check_vma=False,
    )
```

```python
import numpy as np
import jax
import jax.numpy as jnp
from jax import lax
from jax.experimental import pallas as pl
from jax.experimental.pallas import tpu as pltpu
from jax.sharding import Mesh, PartitionSpec as P

momentum_decay = 0.999
step_size = 0.01
SITE = ("z", "core")
GROUP = ("yl", "x")
DEV = ("yh", "yl", "x")
MIB = 1024 * 1024
ACROSS = (((1,), (1,)), ((), ()))


def pair_table():
    freq = np.arange(64)[:, None]
    place = np.arange(64)[None, :]
    factor = np.where(freq == 0, np.sqrt(1.0 / 64.0), np.sqrt(2.0 / 64.0))
    one = factor * np.cos(np.pi * (2.0 * place + 1.0) * freq / 128.0)
    return np.kron(np.eye(2), one).astype(np.float32)


def exact_dot(a, b):
    return jnp.dot(a, b, precision=lax.Precision.HIGHEST, preferred_element_type=jnp.float32)


def params(mib=16):
    return pltpu.CompilerParams(vmem_limit_bytes=mib * MIB)


def pack(tokens, cotangent, groups):
    tok, width = tokens.shape
    part = width // groups
    rows_all = cotangent.shape[1]
    fold = part // rows_all
    extra = tok // fold

    def body(tok_ref, cot_ref, out_ref, sem):
        moves = [
            pltpu.make_async_copy(tok_ref.at[:, g * part:(g + 1) * part], out_ref.at[g, :tok, :], sem.at[g])
            for g in range(groups)
        ]
        for move in moves:
            move.start()
        for g in range(groups):
            for q in range(fold):
                out_ref[g, tok:, q * rows_all:(q + 1) * rows_all] = cot_ref[q * extra:(q + 1) * extra, :]
        for move in moves:
            move.wait()

    return pl.pallas_call(
        body,
        in_specs=[pl.BlockSpec(memory_space=pltpu.HBM), pl.BlockSpec(memory_space=pltpu.VMEM)],
        out_specs=pl.BlockSpec(memory_space=pltpu.VMEM),
        out_shape=jax.ShapeDtypeStruct((groups, tok + extra, part), tokens.dtype),
        scratch_shapes=[pltpu.SemaphoreType.DMA((groups,))],
        compiler_params=params(),
        name="pack",
    )(tokens, cotangent)


def gradient(joined, tok, rows_all):
    groups, high, part = joined.shape
    extra = high - tok
    fold = tok // extra
    cols = 256

    def body(joined_ref, out_ref):
        left = jnp.concatenate(
            [
                joined_ref[k, tok:, q * rows_all:(q + 1) * rows_all]
                for k in range(groups)
                for q in range(fold)
            ],
            axis=0,
        ).T
        for j in range(0, part, cols):
            right = jnp.concatenate([joined_ref[k, :tok, j:j + cols] for k in range(groups)], axis=0)
            out_ref[:, j:j + cols] = jnp.dot(
                left, right, preferred_element_type=jnp.float32
            ).astype(out_ref.dtype)

    return pl.pallas_call(
        body,
        out_shape=jax.ShapeDtypeStruct((rows_all, part), jnp.bfloat16),
        compiler_params=params(),
        name="gradient",
    )(joined)


def raise_and_pick(terms, momentum, keep, table, groups, nz, ncore):
    rows, width = momentum.shape
    part = width // groups
    tiles = part // 128
    share = rows // ncore

    def body(terms_ref, mom_ref, keep_ref, table_ref, out_ref, sent_ref):
        pieces = []
        for g in range(groups):
            grad = terms_ref[g].astype(jnp.float32)
            for k in range(g + groups, terms_ref.shape[0], groups):
                grad = grad + terms_ref[k].astype(jnp.float32)
            raised = momentum_decay * mom_ref[:, g * part:(g + 1) * part] + grad
            pieces += [raised[:, t * 128:(t + 1) * 128] for t in range(tiles)]
        raised = jnp.concatenate(pieces, axis=0)
        both = table_ref[...]
        picked = exact_dot(raised, both.T) * keep_ref[...]
        moment_new = raised - exact_dot(picked, both)
        for j in range(width // 128):
            out_ref[:, j * 128:(j + 1) * 128] = moment_new[j * rows:(j + 1) * rows]
        for t in range(tiles):
            for c in range(ncore):
                starts = [(g * tiles + t) * rows + c * share for g in range(groups)]
                mine = jnp.concatenate([picked[at:at + share] for at in starts], axis=0)
                sent_ref[t * ncore + c] = mine.astype(jnp.bfloat16)

    return pl.pallas_call(
        body,
        out_shape=(
            jax.ShapeDtypeStruct((rows, width), jnp.float32),
            jax.ShapeDtypeStruct((nz * ncore, groups * share, 128), jnp.bfloat16),
        ),
        compiler_params=params(),
        name="raise_and_pick",
    )(terms, momentum, keep, table)


def update(sent, weight, table, groups, copies):
    sites, high, lanes = sent.shape
    rows, width = weight.shape
    part = width // groups
    share = high // groups

    def body(sent_ref, weight_ref, table_ref, out_ref):
        z, first = lax.axis_index("z"), lax.axis_index("core") == 0
        total = sent_ref[0].astype(jnp.float32)
        for s in range(1, sites):
            total = total + sent_ref[s].astype(jnp.float32)
        decoded = exact_dot(total, table_ref[...])
        held = []
        for g in range(groups):
            at = pl.multiple_of(g * part + z * 128, 128)
            tile = weight_ref[:, pl.ds(at, 128)].astype(jnp.float32)
            held.append(jnp.where(first, tile[:share], tile[share:]))
        fresh = (jnp.concatenate(held, axis=0) - step_size * decoded).astype(jnp.bfloat16)
        for c in range(copies):
            out_ref[c] = fresh

    return pl.pallas_call(
        body,
        out_shape=jax.ShapeDtypeStruct((copies, high, lanes), jnp.bfloat16),
        compiler_params=params(),
        name="update",
    )(sent, weight, table)


def project(joined, mine, other, tok):
    groups, _, part = joined.shape
    tiles, half, _ = mine.shape

    def body(tok_ref, mine_ref, other_ref, out_ref, weight_ref):
        @pl.when(pl.program_id(0) == 0)
        def _():
            first = lax.axis_index("core") == 0
            for t in range(tiles):
                a, b = mine_ref[t], other_ref[t]
                weight_ref[:half, t * 128:(t + 1) * 128] = jnp.where(first, a, b)
                weight_ref[half:, t * 128:(t + 1) * 128] = jnp.where(first, b, a)

        for k in range(2):
            out_ref[k] = lax.dot_general(
                tok_ref[k], weight_ref[...], ACROSS, preferred_element_type=jnp.float32
            ).astype(out_ref.dtype)

    whole = pl.BlockSpec((tiles, half, 128), lambda g: (0, 0, 0))
    return pl.pallas_call(
        body,
        grid=(groups // 2,),
        in_specs=[pl.BlockSpec((2, tok, part), lambda g: (g, 0, 0)), whole, whole],
        out_specs=pl.BlockSpec((2, tok, 2 * half), lambda g: (g, 0, 0)),
        out_shape=jax.ShapeDtypeStruct((groups, tok, 2 * half), jnp.bfloat16),
        scratch_shapes=[pltpu.VMEM((2 * half, part), jnp.bfloat16)],
        compiler_params=params(),
        name="project",
    )(joined, mine, other)


def finish(parts, rows, ncore):
    count, tok, rows_all = parts.shape
    share = rows // ncore

    def body(parts_ref, out_ref):
        scores = parts_ref[0].astype(jnp.float32)
        for k in range(1, count):
            scores = scores + parts_ref[k].astype(jnp.float32)
        there = lax.broadcasted_iota(jnp.int32, (rows_all, rows_all), 1)
        here = lax.broadcasted_iota(jnp.int32, (rows_all, rows_all), 0)
        source = there % rows // share * (rows_all // ncore) + there // rows * share + there % share
        order = jnp.where(here == source, 1.0, 0.0).astype(jnp.bfloat16)
        out_ref[...] = jnp.dot(
            scores.astype(jnp.bfloat16), order, preferred_element_type=jnp.float32
        ).astype(jnp.bfloat16)

    return pl.pallas_call(
        body,
        out_shape=jax.ShapeDtypeStruct((tok, rows_all), jnp.bfloat16),
        compiler_params=params(),
        name="finish",
    )(parts)


def exchange(value, axes):
    return lax.all_to_all(value, axes, 0, 0, tiled=True)


def shards(tokens, cotangent, weight, momentum, kept_index):
    nz, ncore, nyh, nyl, nx = (lax.axis_size(name) for name in ("z", "core", "yh", "yl", "x"))
    groups = nyl * nx
    site = lax.axis_index(SITE)
    _, tok, width = tokens.shape
    rows_all = cotangent.shape[2]
    rows = weight.shape[0]
    part = width // groups
    table = jnp.asarray(pair_table())

    joined = exchange(pack(tokens[0], cotangent[0], groups), GROUP)

    tiles = width // 128
    own = lax.dynamic_index_in_dim(kept_index, site, 0, keepdims=False)
    own = own.reshape(rows, tiles, 2, -1) + jnp.array([0, 64], jnp.int32)[None, None, :, None]
    own = own.reshape(rows, tiles, -1).transpose(1, 0, 2)
    keep = jnp.any(own[..., None] == jnp.arange(128, dtype=jnp.int32), axis=2)
    keep = keep.astype(jnp.float32).reshape(tiles * rows, 128)

    partial = gradient(joined, tok, rows_all)
    terms = exchange(partial.reshape(nyh * groups, rows, part), DEV)
    moment_new, sent = raise_and_pick(terms, momentum[0], keep, table, groups, nz, ncore)

    fresh = update(exchange(sent, SITE), weight, table, groups, nz * nyh)
    fresh = exchange(fresh.reshape(nz * nyh * groups, rows // ncore, 128), ("z",) + DEV)
    mine = fresh.reshape(nz, rows_all // ncore, 128)
    other = lax.ppermute(mine, "core", [(0, 1), (1, 0)])
    scores = exchange(project(joined, mine, other, tok), GROUP)
    return (finish(scores, rows, ncore)[None], moment_new[None])


def solution(mesh):
    grid = Mesh(mesh.devices.reshape(8, 2, 4, 2, 4), ("z", "core", "yh", "yl", "x"))
    placed = (
        P(SITE, DEV, None),
        P(SITE, DEV, None),
        P(DEV, None),
        P(SITE, DEV, None),
        P(None, DEV, None, None),
    )
    return jax.shard_map(
        shards,
        mesh=grid,
        in_specs=placed,
        out_specs=(P(SITE, DEV, None), P(SITE, DEV, None)),
        check_vma=False,
    )
```

```python
import numpy as np
import jax
import jax.numpy as jnp
from jax import lax
from jax.experimental import pallas as pl
from jax.experimental.pallas import tpu as pltpu
from jax.sharding import Mesh, PartitionSpec as P

momentum_decay = 0.999
step_size = 0.01
SITE = ("z", "core")
GROUP = ("yl", "x")
DEV = ("yh", "yl", "x")
MIB = 1024 * 1024
ACROSS = (((1,), (1,)), ((), ()))
SIDE = 16


def pair_table():
    freq = np.arange(64)[:, None]
    place = np.arange(64)[None, :]
    factor = np.where(freq == 0, np.sqrt(1.0 / 64.0), np.sqrt(2.0 / 64.0))
    one = factor * np.cos(np.pi * (2.0 * place + 1.0) * freq / 128.0)
    return np.kron(np.eye(2), one).astype(np.float32)


def exact_dot(a, b):
    return jnp.dot(a, b, precision=lax.Precision.HIGHEST, preferred_element_type=jnp.float32)


def iota(shape, axis):
    return lax.broadcasted_iota(jnp.int32, shape, axis)


def params(mib=16):
    return pltpu.CompilerParams(vmem_limit_bytes=mib * MIB)


def pack(tokens, cotangent, momentum, weight, kept, groups):
    tok, width = tokens.shape
    part = width // groups
    rows_all = cotangent.shape[1]
    rows = weight.shape[0]
    fold = part // rows_all
    extra = tok // fold
    _, entries, blocks = kept.shape
    below = extra + SIDE

    def body(tok_ref, cot_ref, mom_ref, weight_ref, kept_ref, out_ref, held_ref, cot_vmem, mom_vmem, weight_vmem,
             spots_ref, in_sem, part_sem, out_sem):
        fetches = [
            pltpu.make_async_copy(tok_ref.at[:, g * part:(g + 1) * part], held_ref.at[g, :tok, :], in_sem.at[g])
            for g in range(groups)
        ]
        sends = [pltpu.make_async_copy(held_ref.at[g], out_ref.at[g], out_sem.at[g]) for g in range(groups)]
        parts = [
            pltpu.make_async_copy(kept_ref.at[lax.axis_index(SITE)], spots_ref, part_sem.at[0]),
            pltpu.make_async_copy(cot_ref, cot_vmem, part_sem.at[1]),
            pltpu.make_async_copy(mom_ref, mom_vmem, part_sem.at[2]),
            pltpu.make_async_copy(weight_ref, weight_vmem, part_sem.at[3]),
        ]
        for fetch in parts + fetches:
            fetch.start()
        for fetch in parts:
            fetch.wait()
        z = lax.axis_index("z")
        spots = spots_ref[...].astype(jnp.float32).T
        unused = jnp.zeros((rows, part - 3 * 128), jnp.float32)
        span = part // 64
        for g in range(groups):
            for q in range(fold):
                held_ref[g, tok:tok + extra, q * rows_all:(q + 1) * rows_all] = cot_vmem[q * extra:(q + 1) * extra, :]
            tile = weight_vmem[:, pl.ds(pl.multiple_of(g * part + z * 128, 128), 128)].astype(jnp.float32)
            low = [spots[g * span + h * rows:g * span + (h + 1) * rows] for h in range(span // rows)]
            low = jnp.concatenate(low + [tile, unused], axis=1)
            side = jnp.concatenate([mom_vmem[:, g * part:(g + 1) * part], low], axis=0)
            held_ref[g, tok + extra:, :] = side.astype(jnp.bfloat16)
        for fetch, send in zip(fetches, sends):
            fetch.wait()
            send.start()
        for send in sends:
            send.wait()

    anywhere = pl.BlockSpec(memory_space=pl.ANY)
    return pl.pallas_call(
        body,
        in_specs=[anywhere] * 5,
        out_specs=anywhere,
        out_shape=jax.ShapeDtypeStruct((groups, tok + below, part), tokens.dtype),
        scratch_shapes=[
            pltpu.VMEM((groups, tok + below, part), tokens.dtype),
            pltpu.VMEM((tok, rows_all), cotangent.dtype),
            pltpu.VMEM((rows, width), jnp.float32),
            pltpu.VMEM((rows, width), weight.dtype),
            pltpu.VMEM((entries, blocks), jnp.int32),
            pltpu.SemaphoreType.DMA((groups,)),
            pltpu.SemaphoreType.DMA((4,)),
            pltpu.SemaphoreType.DMA((groups,)),
        ],
        compiler_params=params(62),
        name="pack",
    )(tokens, cotangent, momentum, weight, kept)


def gradient(joined, tok, rows_all):
    groups, high, part = joined.shape
    extra = high - tok - SIDE
    fold = tok // extra
    cols = 256

    def body(joined_ref, out_ref):
        left = jnp.concatenate(
            [
                joined_ref[k, tok:tok + extra, q * rows_all:(q + 1) * rows_all]
                for k in range(groups)
                for q in range(fold)
            ],
            axis=0,
        ).T
        for j in range(0, part, cols):
            right = jnp.concatenate([joined_ref[k, :tok, j:j + cols] for k in range(groups)], axis=0)
            out_ref[:, j:j + cols] = jnp.dot(
                left, right, preferred_element_type=jnp.float32
            ).astype(out_ref.dtype)

    return pl.pallas_call(
        body,
        out_shape=jax.ShapeDtypeStruct((rows_all, part), jnp.bfloat16),
        compiler_params=params(),
        name="gradient",
    )(joined)


def raise_and_pick(terms, joined, table, sites, rows_all, nx):
    nyh, band, part = terms.shape
    groups, high, _ = joined.shape
    tiles = part // 128
    rows = band // groups
    fold = part // rows_all
    span = part // 64

    def body(terms_ref, side_ref, table_ref, sent_ref, change_ref, held_ref, keep_ref, moment_ref):
        core = lax.axis_index("core")
        freq = iota((64, 128), 0).astype(jnp.float32)
        gather = iota((rows, 128), 0) == iota((rows, 128), 1) // (128 // rows)
        gather = jnp.where(gather, 1.0, 0.0).astype(jnp.bfloat16)
        for g in range(groups):
            side = side_ref[g].astype(jnp.float32)
            marks = []
            for b in range(span):
                line = side[rows + b % rows:rows + b % rows + 1, b // rows * 128:(b // rows + 1) * 128]
                marks.append(jnp.where(line == freq, 1.0, 0.0).astype(jnp.bfloat16))
            keep = lax.dot_general(
                gather, jnp.concatenate(marks, axis=0), ACROSS, preferred_element_type=jnp.float32
            )
            for t in range(tiles):
                at = t * band + g * rows
                keep_ref[at:at + rows, :] = keep[:, t * 128:(t + 1) * 128]
                moment_ref[at:at + rows, :] = momentum_decay * side[:rows, t * 128:(t + 1) * 128]
        for x in range(nx):
            side = side_ref[core * nx + x].astype(jnp.float32)
            held_ref[x * rows:(x + 1) * rows, :] = side[rows:2 * rows, span // rows * 128:(span // rows + 1) * 128]

        grad = terms_ref[0].astype(jnp.float32)
        for k in range(1, nyh):
            grad = grad + terms_ref[k].astype(jnp.float32)
        grad = jnp.concatenate([grad[:, t * 128:(t + 1) * 128] for t in range(tiles)], axis=0)
        both = table_ref[...]
        picked = exact_dot(moment_ref[...] + grad, both.T) * keep_ref[...]
        sent_ref[...] = picked.astype(jnp.bfloat16).reshape(sent_ref.shape)
        change = grad - exact_dot(picked, both)
        for g in range(groups):
            pieces = []
            for q in range(fold):
                across = []
                for t in range(q * tiles // fold, (q + 1) * tiles // fold):
                    at = t * band + g * rows
                    across.append(change[at:at + rows])
                pieces.append(jnp.concatenate(across, axis=1))
            change_ref[g] = jnp.concatenate(pieces, axis=0).astype(jnp.bfloat16)

    def whole(*shape):
        return pl.BlockSpec(shape, lambda i: (0,) * len(shape))

    share = tiles * band // sites
    return pl.pallas_call(
        body,
        grid=(1,),
        in_specs=[
            whole(nyh, band, part),
            pl.BlockSpec((groups, SIDE, part), lambda i: (0, high // SIDE - 1, 0)),
            whole(128, 128),
        ],
        out_specs=(whole(sites, share, 128), whole(groups, fold * rows, rows_all), whole(nx * rows, 128)),
        out_shape=(
            jax.ShapeDtypeStruct((sites, share, 128), jnp.bfloat16),
            jax.ShapeDtypeStruct((groups, fold * rows, rows_all), jnp.bfloat16),
            jax.ShapeDtypeStruct((nx * rows, 128), jnp.float32),
        ),
        scratch_shapes=[pltpu.VMEM((tiles * band, 128), jnp.float32)] * 2,
        compiler_params=params(),
        name="raise_and_pick",
    )(terms, joined, table)


def update(sent, held, table, copies):
    sites, high, lanes = sent.shape

    def body(sent_ref, held_ref, table_ref, out_ref):
        total = sent_ref[0].astype(jnp.float32)
        for s in range(1, sites):
            total = total + sent_ref[s].astype(jnp.float32)
        fresh = (held_ref[...] - step_size * exact_dot(total, table_ref[...])).astype(jnp.bfloat16)
        for c in range(copies):
            out_ref[c] = fresh

    return pl.pallas_call(
        body,
        out_shape=jax.ShapeDtypeStruct((copies, high, lanes), jnp.bfloat16),
        compiler_params=params(),
        name="update",
    )(sent, held, table)


def project(joined, mine, other, change, tok):
    groups, _, part = joined.shape
    tiles, nyh, share, _ = mine.shape
    rows_all = 2 * nyh * share
    extra = change.shape[1]

    def body(joined_ref, mine_ref, other_ref, change_ref, out_ref):
        first = lax.axis_index("core") == 0
        weight = []
        for t in range(tiles):
            bands = []
            for y in range(nyh):
                a, b = mine_ref[t, y], other_ref[t, y]
                bands += [jnp.where(first, a, b), jnp.where(first, b, a)]
            weight.append(jnp.concatenate(bands, axis=0))
        weight = jnp.concatenate(weight, axis=1)
        for k in range(groups):
            out_ref[k, :tok, :] = lax.dot_general(
                joined_ref[k, :tok, :], weight, ACROSS, preferred_element_type=jnp.float32
            ).astype(out_ref.dtype)
            out_ref[k, tok:, :] = change_ref[k]

    return pl.pallas_call(
        body,
        out_shape=jax.ShapeDtypeStruct((groups, tok + extra, rows_all), jnp.bfloat16),
        compiler_params=params(),
        name="project",
    )(joined, mine, other, change)


def finish(parts, momentum, tok):
    groups, high, rows_all = parts.shape
    rows, width = momentum.shape
    part = width // groups

    def body(parts_ref, mom_ref, scores_ref, out_ref):
        scores = parts_ref[0, :tok, :].astype(jnp.float32)
        for k in range(1, groups):
            scores = scores + parts_ref[k, :tok, :].astype(jnp.float32)
        scores_ref[...] = scores.astype(jnp.bfloat16)
        for g in range(groups):
            change = parts_ref[g, tok:, :].astype(jnp.float32)
            for q in range(part // rows_all):
                at = g * part + q * rows_all
                out_ref[:, at:at + rows_all] = (
                    momentum_decay * mom_ref[:, at:at + rows_all] + change[q * rows:(q + 1) * rows]
                )

    return pl.pallas_call(
        body,
        out_shape=(
            jax.ShapeDtypeStruct((tok, rows_all), jnp.bfloat16),
            jax.ShapeDtypeStruct((rows, width), jnp.float32),
        ),
        compiler_params=params(),
        name="finish",
    )(parts, momentum)


def exchange(value, axes):
    return lax.all_to_all(value, axes, 0, 0, tiled=True)


def shards(tokens, cotangent, weight, momentum, kept_index):
    nz, ncore, nyh, nyl, nx = (lax.axis_size(name) for name in ("z", "core", "yh", "yl", "x"))
    groups = nyl * nx
    sites = nz * ncore
    _, tok, width = tokens.shape
    rows_all = cotangent.shape[2]
    rows = weight.shape[0]
    part = width // groups
    band = rows_all // nyh
    table = jnp.asarray(pair_table())

    kept = kept_index.transpose(0, 1, 3, 2).reshape(sites, -1, width // 64)
    joined = exchange(pack(tokens[0], cotangent[0], momentum[0], weight, kept, groups), GROUP)

    partial = gradient(joined, tok, rows_all)
    terms = exchange(partial.reshape(nyh, band, part), "yh")
    sent, change, held = raise_and_pick(terms, joined, table, sites, rows_all, nx)

    fresh = update(exchange(sent, SITE), held, table, nz * nyh)
    mine = exchange(fresh, ("z", "yh")).reshape(nz, nyh, band // ncore, 128)
    other = lax.ppermute(mine, "core", [(0, 1), (1, 0)])
    scores, moment_new = finish(exchange(project(joined, mine, other, change, tok), GROUP), momentum[0], tok)
    return (scores[None], moment_new[None])


def solution(mesh):
    grid = Mesh(mesh.devices.reshape(8, 2, 4, 2, 4), ("z", "core", "yh", "yl", "x"))
    placed = (
        P(SITE, DEV, None),
        P(SITE, DEV, None),
        P(DEV, None),
        P(SITE, DEV, None),
        P(None, DEV, None, None),
    )
    return jax.shard_map(
        shards,
        mesh=grid,
        in_specs=placed,
        out_specs=(P(SITE, DEV, None), P(SITE, DEV, None)),
        check_vma=False,
    )
```

```python
import numpy as np
import jax
import jax.numpy as jnp
from jax import lax
from jax.experimental import pallas as pl
from jax.experimental.pallas import tpu as pltpu
from jax.sharding import Mesh, PartitionSpec as P

momentum_decay = 0.999
step_size = 0.01
SITE = ("z", "core")
GROUP = ("yl", "x")
DEV = ("yh", "yl", "x")
MIB = 1024 * 1024
ACROSS = (((1,), (1,)), ((), ()))
SIDE = 16


def pair_table():
    freq = np.arange(64)[:, None]
    place = np.arange(64)[None, :]
    factor = np.where(freq == 0, np.sqrt(1.0 / 64.0), np.sqrt(2.0 / 64.0))
    one = factor * np.cos(np.pi * (2.0 * place + 1.0) * freq / 128.0)
    return np.kron(np.eye(2), one).astype(np.float32)


def exact_dot(a, b):
    return jnp.dot(a, b, precision=lax.Precision.HIGHEST, preferred_element_type=jnp.float32)


def iota(shape, axis):
    return lax.broadcasted_iota(jnp.int32, shape, axis)


def halves(a):
    high = a.astype(jnp.bfloat16)
    return high, (a - high.astype(jnp.float32)).astype(jnp.bfloat16)


def close_dot(a, b):
    (a_high, a_low), (b_high, b_low) = halves(a), halves(b)

    def dot(p, q):
        return jnp.dot(p, q, preferred_element_type=jnp.float32)

    return dot(a_high, b_high) + (dot(a_high, b_low) + dot(a_low, b_high))


def params(mib=16):
    return pltpu.CompilerParams(vmem_limit_bytes=mib * MIB)


def pack(tokens, cotangent, momentum, weight, kept, groups):
    tok, width = tokens.shape
    part = width // groups
    rows_all = cotangent.shape[1]
    rows = weight.shape[0]
    fold = part // rows_all
    extra = tok // fold
    _, entries, blocks = kept.shape
    below = extra + SIDE

    def body(tok_ref, cot_ref, mom_ref, weight_ref, kept_ref, out_ref, held_ref, cot_vmem, mom_vmem, weight_vmem,
             spots_ref, in_sem, part_sem, out_sem):
        fetches = [
            pltpu.make_async_copy(tok_ref.at[:, g * part:(g + 1) * part], held_ref.at[g, :tok, :], in_sem.at[g])
            for g in range(groups)
        ]
        sends = [pltpu.make_async_copy(held_ref.at[g], out_ref.at[g], out_sem.at[g]) for g in range(groups)]
        parts = [
            pltpu.make_async_copy(kept_ref.at[lax.axis_index(SITE)], spots_ref, part_sem.at[0]),
            pltpu.make_async_copy(cot_ref, cot_vmem, part_sem.at[1]),
            pltpu.make_async_copy(mom_ref, mom_vmem, part_sem.at[2]),
            pltpu.make_async_copy(weight_ref, weight_vmem, part_sem.at[3]),
        ]
        for fetch in parts + fetches:
            fetch.start()
        for fetch in parts:
            fetch.wait()
        z = lax.axis_index("z")
        spots = spots_ref[...].astype(jnp.float32).T
        unused = jnp.zeros((rows, part - 3 * 128), jnp.float32)
        span = part // 64
        for g in range(groups):
            for q in range(fold):
                held_ref[g, tok:tok + extra, q * rows_all:(q + 1) * rows_all] = cot_vmem[q * extra:(q + 1) * extra, :]
            tile = weight_vmem[:, pl.ds(pl.multiple_of(g * part + z * 128, 128), 128)].astype(jnp.float32)
            low = [spots[g * span + h * rows:g * span + (h + 1) * rows] for h in range(span // rows)]
            low = jnp.concatenate(low + [tile, unused], axis=1)
            side = jnp.concatenate([mom_vmem[:, g * part:(g + 1) * part], low], axis=0)
            held_ref[g, tok + extra:, :] = side.astype(jnp.bfloat16)
            fetches[g].wait()
            sends[g].start()
        for send in sends:
            send.wait()

    anywhere = pl.BlockSpec(memory_space=pl.ANY)
    return pl.pallas_call(
        body,
        in_specs=[anywhere] * 5,
        out_specs=anywhere,
        out_shape=jax.ShapeDtypeStruct((groups, tok + below, part), tokens.dtype),
        scratch_shapes=[
            pltpu.VMEM((groups, tok + below, part), tokens.dtype),
            pltpu.VMEM((tok, rows_all), cotangent.dtype),
            pltpu.VMEM((rows, width), jnp.float32),
            pltpu.VMEM((rows, width), weight.dtype),
            pltpu.VMEM((entries, blocks), jnp.int32),
            pltpu.SemaphoreType.DMA((groups,)),
            pltpu.SemaphoreType.DMA((4,)),
            pltpu.SemaphoreType.DMA((groups,)),
        ],
        compiler_params=params(62),
        name="pack",
    )(tokens, cotangent, momentum, weight, kept)


def gradient(joined, tok, rows_all):
    groups, high, part = joined.shape
    extra = high - tok - SIDE
    fold = tok // extra
    cols = 256

    def body(joined_ref, out_ref):
        left = jnp.concatenate(
            [
                joined_ref[k, tok:tok + extra, q * rows_all:(q + 1) * rows_all]
                for k in range(groups)
                for q in range(fold)
            ],
            axis=0,
        ).T
        for j in range(0, part, cols):
            right = jnp.concatenate([joined_ref[k, :tok, j:j + cols] for k in range(groups)], axis=0)
            out_ref[:, j:j + cols] = jnp.dot(
                left, right, preferred_element_type=jnp.float32
            ).astype(out_ref.dtype)

    return pl.pallas_call(
        body,
        out_shape=jax.ShapeDtypeStruct((rows_all, part), jnp.bfloat16),
        compiler_params=params(),
        name="gradient",
    )(joined)


def raise_and_pick(terms, joined, table, sites, rows_all, nx):
    nyh, band, part = terms.shape
    groups, high, _ = joined.shape
    tiles = part // 128
    rows = band // groups
    fold = part // rows_all
    span = part // 64

    def body(terms_ref, side_ref, table_ref, sent_ref, change_ref, held_ref, keep_ref, moment_ref):
        core = lax.axis_index("core")
        freq = iota((64, 128), 0).astype(jnp.float32)
        gather = iota((rows, 128), 0) == iota((rows, 128), 1) // (128 // rows)
        gather = jnp.where(gather, 1.0, 0.0).astype(jnp.bfloat16)
        for g in range(groups):
            side = side_ref[g].astype(jnp.float32)
            marks = []
            for b in range(span):
                line = side[rows + b % rows:rows + b % rows + 1, b // rows * 128:(b // rows + 1) * 128]
                marks.append(jnp.where(line == freq, 1.0, 0.0).astype(jnp.bfloat16))
            keep = lax.dot_general(
                gather, jnp.concatenate(marks, axis=0), ACROSS, preferred_element_type=jnp.float32
            )
            for t in range(tiles):
                at = t * band + g * rows
                keep_ref[at:at + rows, :] = keep[:, t * 128:(t + 1) * 128]
                moment_ref[at:at + rows, :] = momentum_decay * side[:rows, t * 128:(t + 1) * 128]
        for x in range(nx):
            side = side_ref[core * nx + x].astype(jnp.float32)
            held_ref[x * rows:(x + 1) * rows, :] = side[rows:2 * rows, span // rows * 128:(span // rows + 1) * 128]

        grad = terms_ref[0].astype(jnp.float32)
        for k in range(1, nyh):
            grad = grad + terms_ref[k].astype(jnp.float32)
        grad = jnp.concatenate([grad[:, t * 128:(t + 1) * 128] for t in range(tiles)], axis=0)
        both = table_ref[...]
        picked = close_dot(moment_ref[...] + grad, both.T) * keep_ref[...]
        sent_ref[...] = picked.astype(jnp.bfloat16).reshape(sent_ref.shape)
        change = grad - close_dot(picked, both)
        for g in range(groups):
            pieces = []
            for q in range(fold):
                across = []
                for t in range(q * tiles // fold, (q + 1) * tiles // fold):
                    at = t * band + g * rows
                    across.append(change[at:at + rows])
                pieces.append(jnp.concatenate(across, axis=1))
            change_ref[g] = jnp.concatenate(pieces, axis=0).astype(jnp.bfloat16)

    def whole(*shape):
        return pl.BlockSpec(shape, lambda i: (0,) * len(shape))

    share = tiles * band // sites
    return pl.pallas_call(
        body,
        grid=(1,),
        in_specs=[
            whole(nyh, band, part),
            pl.BlockSpec((groups, SIDE, part), lambda i: (0, high // SIDE - 1, 0)),
            whole(128, 128),
        ],
        out_specs=(whole(sites, share, 128), whole(groups, fold * rows, rows_all), whole(nx * rows, 128)),
        out_shape=(
            jax.ShapeDtypeStruct((sites, share, 128), jnp.bfloat16),
            jax.ShapeDtypeStruct((groups, fold * rows, rows_all), jnp.bfloat16),
            jax.ShapeDtypeStruct((nx * rows, 128), jnp.float32),
        ),
        scratch_shapes=[pltpu.VMEM((tiles * band, 128), jnp.float32)] * 2,
        compiler_params=params(),
        name="raise_and_pick",
    )(terms, joined, table)


def update(sent, held, table, copies):
    sites, high, lanes = sent.shape

    def body(sent_ref, held_ref, table_ref, out_ref):
        total = sent_ref[0].astype(jnp.float32)
        for s in range(1, sites):
            total = total + sent_ref[s].astype(jnp.float32)
        fresh = (held_ref[...] - step_size * exact_dot(total, table_ref[...])).astype(jnp.bfloat16)
        for c in range(copies):
            out_ref[c] = fresh

    return pl.pallas_call(
        body,
        out_shape=jax.ShapeDtypeStruct((copies, high, lanes), jnp.bfloat16),
        compiler_params=params(),
        name="update",
    )(sent, held, table)


def project(joined, mine, other, change, tok):
    groups, _, part = joined.shape
    tiles, nyh, share, _ = mine.shape
    rows_all = 2 * nyh * share
    extra = change.shape[1]

    def body(joined_ref, mine_ref, other_ref, change_ref, out_ref):
        first = lax.axis_index("core") == 0
        weight = []
        for t in range(tiles):
            bands = []
            for y in range(nyh):
                a, b = mine_ref[t, y], other_ref[t, y]
                bands += [jnp.where(first, a, b), jnp.where(first, b, a)]
            weight.append(jnp.concatenate(bands, axis=0))
        weight = jnp.concatenate(weight, axis=1)
        weight = weight.T
        for k in range(0, groups, 2):
            both = jnp.concatenate([joined_ref[k, :tok, :], joined_ref[k + 1, :tok, :]], axis=0)
            both = jnp.dot(both, weight, preferred_element_type=jnp.float32).astype(out_ref.dtype)
            out_ref[k, :tok, :] = both[:tok]
            out_ref[k + 1, :tok, :] = both[tok:]
        for k in range(groups):
            out_ref[k, tok:, :] = change_ref[k]

    return pl.pallas_call(
        body,
        out_shape=jax.ShapeDtypeStruct((groups, tok + extra, rows_all), jnp.bfloat16),
        compiler_params=params(),
        name="project",
    )(joined, mine, other, change)


def finish(parts, momentum, tok):
    groups, high, rows_all = parts.shape
    rows, width = momentum.shape
    part = width // groups

    def body(parts_ref, mom_ref, scores_ref, out_ref):
        scores = parts_ref[0, :tok, :].astype(jnp.float32)
        for k in range(1, groups):
            scores = scores + parts_ref[k, :tok, :].astype(jnp.float32)
        scores_ref[...] = scores.astype(jnp.bfloat16)
        for g in range(groups):
            change = parts_ref[g, tok:, :].astype(jnp.float32)
            for q in range(part // rows_all):
                at = g * part + q * rows_all
                out_ref[:, at:at + rows_all] = (
                    momentum_decay * mom_ref[:, at:at + rows_all] + change[q * rows:(q + 1) * rows]
                )

    return pl.pallas_call(
        body,
        out_shape=(
            jax.ShapeDtypeStruct((tok, rows_all), jnp.bfloat16),
            jax.ShapeDtypeStruct((rows, width), jnp.float32),
        ),
        compiler_params=params(),
        name="finish",
    )(parts, momentum)


def exchange(value, axes):
    return lax.all_to_all(value, axes, 0, 0, tiled=True)


def shards(tokens, cotangent, weight, momentum, kept_index):
    nz, ncore, nyh, nyl, nx = (lax.axis_size(name) for name in ("z", "core", "yh", "yl", "x"))
    groups = nyl * nx
    sites = nz * ncore
    _, tok, width = tokens.shape
    rows_all = cotangent.shape[2]
    rows = weight.shape[0]
    part = width // groups
    band = rows_all // nyh
    table = jnp.asarray(pair_table())

    kept = kept_index.transpose(0, 1, 3, 2).reshape(sites, -1, width // 64)
    joined = exchange(pack(tokens[0], cotangent[0], momentum[0], weight, kept, groups), GROUP)

    partial = gradient(joined, tok, rows_all)
    terms = exchange(partial.reshape(nyh, band, part), "yh")
    sent, change, held = raise_and_pick(terms, joined, table, sites, rows_all, nx)

    fresh = update(exchange(sent, SITE), held, table, nz * nyh)
    mine = exchange(fresh, ("z", "yh")).reshape(nz, nyh, band // ncore, 128)
    other = lax.ppermute(mine, "core", [(0, 1), (1, 0)])
    scores, moment_new = finish(exchange(project(joined, mine, other, change, tok), GROUP), momentum[0], tok)
    return (scores[None], moment_new[None])


def solution(mesh):
    grid = Mesh(mesh.devices.reshape(8, 2, 4, 2, 4), ("z", "core", "yh", "yl", "x"))
    placed = (
        P(SITE, DEV, None),
        P(SITE, DEV, None),
        P(DEV, None),
        P(SITE, DEV, None),
        P(None, DEV, None, None),
    )
    return jax.shard_map(
        shards,
        mesh=grid,
        in_specs=placed,
        out_specs=(P(SITE, DEV, None), P(SITE, DEV, None)),
        check_vma=False,
    )
```

```python
import numpy as np
import jax
import jax.numpy as jnp
from jax import lax
from jax.experimental import pallas as pl
from jax.experimental.pallas import tpu as pltpu
from jax.sharding import Mesh, PartitionSpec as P

momentum_decay = 0.999
step_size = 0.01
SITE = ("z", "core")
GROUP = ("yl", "x")
DEV = ("yh", "yl", "x")
MIB = 1024 * 1024
ACROSS = (((1,), (1,)), ((), ()))
SIDE = 16


def pair_table():
    freq = np.arange(64)[:, None]
    place = np.arange(64)[None, :]
    factor = np.where(freq == 0, np.sqrt(1.0 / 64.0), np.sqrt(2.0 / 64.0))
    one = factor * np.cos(np.pi * (2.0 * place + 1.0) * freq / 128.0)
    return np.kron(np.eye(2), one).astype(np.float32)


def exact_dot(a, b):
    return jnp.dot(a, b, precision=lax.Precision.HIGHEST, preferred_element_type=jnp.float32)


def iota(shape, axis):
    return lax.broadcasted_iota(jnp.int32, shape, axis)


def halves(a):
    high = a.astype(jnp.bfloat16)
    return high, (a - high.astype(jnp.float32)).astype(jnp.bfloat16)


def close_dot(a, b):
    (a_high, a_low), (b_high, b_low) = halves(a), halves(b)

    def dot(p, q):
        return jnp.dot(p, q, preferred_element_type=jnp.float32)

    return dot(a_high, b_high) + (dot(a_high, b_low) + dot(a_low, b_high))


def params(mib=16):
    return pltpu.CompilerParams(vmem_limit_bytes=mib * MIB)


def pack_all(tokens, cotangent, momentum, weight, kept, groups):
    tok, width = tokens.shape
    part = width // groups
    rows_all = cotangent.shape[1]
    rows = weight.shape[0]
    fold = part // rows_all
    extra = tok // fold
    _, entries, blocks = kept.shape
    below = extra + SIDE

    def body(tok_ref, cot_ref, mom_ref, weight_ref, kept_ref, out_ref, held_ref, cot_vmem, mom_vmem, weight_vmem,
             spots_ref, in_sem, part_sem, out_sem):
        fetches = [
            pltpu.make_async_copy(tok_ref.at[:, g * part:(g + 1) * part], held_ref.at[g, :tok, :], in_sem.at[g])
            for g in range(groups)
        ]
        sends = [pltpu.make_async_copy(held_ref.at[g], out_ref.at[g], out_sem.at[g]) for g in range(groups)]
        parts = [
            pltpu.make_async_copy(kept_ref.at[lax.axis_index(SITE)], spots_ref, part_sem.at[0]),
            pltpu.make_async_copy(cot_ref, cot_vmem, part_sem.at[1]),
            pltpu.make_async_copy(mom_ref, mom_vmem, part_sem.at[2]),
            pltpu.make_async_copy(weight_ref, weight_vmem, part_sem.at[3]),
        ]
        for fetch in parts + fetches:
            fetch.start()
        for fetch in parts:
            fetch.wait()
        z = lax.axis_index("z")
        spots = spots_ref[...].astype(jnp.float32).T
        unused = jnp.zeros((rows, part - 3 * 128), jnp.float32)
        span = part // 64
        for g in range(groups):
            for q in range(fold):
                held_ref[g, tok:tok + extra, q * rows_all:(q + 1) * rows_all] = cot_vmem[q * extra:(q + 1) * extra, :]
            tile = weight_vmem[:, pl.ds(pl.multiple_of(g * part + z * 128, 128), 128)].astype(jnp.float32)
            low = [spots[g * span + h * rows:g * span + (h + 1) * rows] for h in range(span // rows)]
            low = jnp.concatenate(low + [tile, unused], axis=1)
            side = jnp.concatenate([mom_vmem[:, g * part:(g + 1) * part], low], axis=0)
            held_ref[g, tok + extra:, :] = side.astype(jnp.bfloat16)
            fetches[g].wait()
            sends[g].start()
        for send in sends:
            send.wait()

    anywhere = pl.BlockSpec(memory_space=pl.ANY)
    return pl.pallas_call(
        body,
        in_specs=[anywhere] * 5,
        out_specs=anywhere,
        out_shape=jax.ShapeDtypeStruct((groups, tok + below, part), tokens.dtype),
        scratch_shapes=[
            pltpu.VMEM((groups, tok + below, part), tokens.dtype),
            pltpu.VMEM((tok, rows_all), cotangent.dtype),
            pltpu.VMEM((rows, width), jnp.float32),
            pltpu.VMEM((rows, width), weight.dtype),
            pltpu.VMEM((entries, blocks), jnp.int32),
            pltpu.SemaphoreType.DMA((groups,)),
            pltpu.SemaphoreType.DMA((4,)),
            pltpu.SemaphoreType.DMA((groups,)),
        ],
        compiler_params=params(62),
        name="pack_all",
    )(tokens, cotangent, momentum, weight, kept)


def split_tokens(tokens, groups):
    tok, width = tokens.shape
    part = width // groups

    def body(tok_ref, out_ref, sem):
        moves = [
            pltpu.make_async_copy(tok_ref.at[:, g * part:(g + 1) * part], out_ref.at[g], sem.at[g])
            for g in range(groups)
        ]
        for move in moves:
            move.start()
        for move in moves:
            move.wait()

    return pl.pallas_call(
        body,
        in_specs=[pl.BlockSpec(memory_space=pl.ANY)],
        out_specs=pl.BlockSpec(memory_space=pltpu.VMEM),
        out_shape=jax.ShapeDtypeStruct((groups, tok, part), tokens.dtype),
        scratch_shapes=[pltpu.SemaphoreType.DMA((groups,))],
        compiler_params=params(),
        name="split_tokens",
    )(tokens)


def pack_rest(cotangent, momentum, weight, kept, groups):
    rows, width = momentum.shape
    part = width // groups
    tok, rows_all = cotangent.shape
    fold = part // rows_all
    extra = tok // fold
    _, entries, blocks = kept.shape

    def body(cot_ref, mom_ref, weight_ref, kept_ref, out_ref, cot_vmem, mom_vmem, weight_vmem, spots_ref, sem):
        parts = [
            pltpu.make_async_copy(kept_ref.at[lax.axis_index(SITE)], spots_ref, sem.at[0]),
            pltpu.make_async_copy(mom_ref, mom_vmem, sem.at[1]),
            pltpu.make_async_copy(weight_ref, weight_vmem, sem.at[2]),
            pltpu.make_async_copy(cot_ref, cot_vmem, sem.at[3]),
        ]
        for fetch in parts:
            fetch.start()
        for fetch in parts:
            fetch.wait()
        z = lax.axis_index("z")
        spots = spots_ref[...].astype(jnp.float32).T
        unused = jnp.zeros((rows, part - 3 * 128), jnp.float32)
        span = part // 64
        for g in range(groups):
            tile = weight_vmem[:, pl.ds(pl.multiple_of(g * part + z * 128, 128), 128)].astype(jnp.float32)
            low = [spots[g * span + h * rows:g * span + (h + 1) * rows] for h in range(span // rows)]
            low = jnp.concatenate(low + [tile, unused], axis=1)
            side = jnp.concatenate([mom_vmem[:, g * part:(g + 1) * part], low], axis=0)
            for q in range(fold):
                out_ref[g, :extra, q * rows_all:(q + 1) * rows_all] = cot_vmem[q * extra:(q + 1) * extra, :]
            out_ref[g, extra:, :] = side.astype(jnp.bfloat16)

    anywhere = pl.BlockSpec(memory_space=pl.ANY)
    return pl.pallas_call(
        body,
        in_specs=[anywhere] * 4,
        out_specs=pl.BlockSpec(memory_space=pltpu.VMEM),
        out_shape=jax.ShapeDtypeStruct((groups, extra + SIDE, part), jnp.bfloat16),
        scratch_shapes=[
            pltpu.VMEM((tok, rows_all), cotangent.dtype),
            pltpu.VMEM((rows, width), jnp.float32),
            pltpu.VMEM((rows, width), weight.dtype),
            pltpu.VMEM((entries, blocks), jnp.int32),
            pltpu.SemaphoreType.DMA((4,)),
        ],
        compiler_params=params(),
        name="pack_rest",
    )(cotangent, momentum, weight, kept)


def follow(value, before):
    def body(value_ref, before_ref, out_ref):
        pass

    anywhere = pl.BlockSpec(memory_space=pl.ANY)
    return pl.pallas_call(
        body,
        in_specs=[anywhere] * 2,
        out_specs=anywhere,
        out_shape=jax.ShapeDtypeStruct(value.shape, value.dtype),
        input_output_aliases={0: 0},
        compiler_params=params(),
        name="follow",
    )(value, before)


def gradient(arrays, tok, rows_all):
    groups, _, part = arrays[0].shape
    fold = part // rows_all
    extra = tok // fold
    cols = 256
    start = tok if len(arrays) == 1 else 0

    def body(*refs):
        tok_ref, rest_ref = refs[0], refs[len(arrays) - 1]
        out_ref, tok_out, side_out, sem = refs[len(arrays):]
        moves = [
            pltpu.make_async_copy(tok_ref.at[:, :tok, :], tok_out, sem.at[0]),
            pltpu.make_async_copy(rest_ref.at[:, start + extra:, :], side_out, sem.at[1]),
        ]
        for move in moves:
            move.start()
        left = jnp.concatenate(
            [
                rest_ref[k, start:start + extra, q * rows_all:(q + 1) * rows_all]
                for k in range(groups)
                for q in range(fold)
            ],
            axis=0,
        ).T
        for j in range(0, part, cols):
            right = jnp.concatenate([tok_ref[k, :tok, j:j + cols] for k in range(groups)], axis=0)
            out_ref[:, j:j + cols] = jnp.dot(
                left, right, preferred_element_type=jnp.float32
            ).astype(out_ref.dtype)
        for move in moves:
            move.wait()

    whole = pl.BlockSpec(memory_space=pltpu.VMEM)
    anywhere = pl.BlockSpec(memory_space=pl.ANY)
    return pl.pallas_call(
        body,
        in_specs=[whole] * len(arrays),
        out_specs=(whole, anywhere, anywhere),
        out_shape=(
            jax.ShapeDtypeStruct((rows_all, part), jnp.bfloat16),
            jax.ShapeDtypeStruct((groups, tok, part), jnp.bfloat16),
            jax.ShapeDtypeStruct((groups, SIDE, part), jnp.bfloat16),
        ),
        scratch_shapes=[pltpu.SemaphoreType.DMA((2,))],
        compiler_params=params(),
        name="gradient",
    )(*arrays)


def raise_and_pick(terms, side, held_tokens, table, sites, rows_all, nx):
    nyh, band, part = terms.shape
    groups = side.shape[0]
    tiles = part // 128
    rows = band // groups
    fold = part // rows_all
    span = part // 64

    def body(terms_hbm, side_hbm, tok_hbm, table_ref, sent_ref, change_ref, held_ref, tok_ref, keep_ref, moment_ref,
             terms_ref, side_ref, sem):
        fetches = [
            pltpu.make_async_copy(side_hbm, side_ref, sem.at[0]),
            pltpu.make_async_copy(terms_hbm, terms_ref, sem.at[1]),
            pltpu.make_async_copy(tok_hbm, tok_ref, sem.at[2]),
        ]
        for fetch in fetches:
            fetch.start()
        core = lax.axis_index("core")
        fetches[0].wait()
        freq = iota((64, 128), 0).astype(jnp.float32)
        gather = iota((rows, 128), 0) == iota((rows, 128), 1) // (128 // rows)
        gather = jnp.where(gather, 1.0, 0.0).astype(jnp.bfloat16)
        for g in range(groups):
            side = side_ref[g].astype(jnp.float32)
            marks = []
            for b in range(span):
                line = side[rows + b % rows:rows + b % rows + 1, b // rows * 128:(b // rows + 1) * 128]
                marks.append(jnp.where(line == freq, 1.0, 0.0).astype(jnp.bfloat16))
            keep = lax.dot_general(
                gather, jnp.concatenate(marks, axis=0), ACROSS, preferred_element_type=jnp.float32
            )
            for t in range(tiles):
                at = t * band + g * rows
                keep_ref[at:at + rows, :] = keep[:, t * 128:(t + 1) * 128]
                moment_ref[at:at + rows, :] = momentum_decay * side[:rows, t * 128:(t + 1) * 128]
        for x in range(nx):
            side = side_ref[core * nx + x].astype(jnp.float32)
            held_ref[x * rows:(x + 1) * rows, :] = side[rows:2 * rows, span // rows * 128:(span // rows + 1) * 128]

        fetches[1].wait()
        grad = terms_ref[0].astype(jnp.float32)
        for k in range(1, nyh):
            grad = grad + terms_ref[k].astype(jnp.float32)
        grad = jnp.concatenate([grad[:, t * 128:(t + 1) * 128] for t in range(tiles)], axis=0)
        both = table_ref[...]
        picked = close_dot(moment_ref[...] + grad, both.T) * keep_ref[...]
        sent_ref[...] = picked.astype(jnp.bfloat16).reshape(sent_ref.shape)
        change = grad - close_dot(picked, both)
        for g in range(groups):
            pieces = []
            for q in range(fold):
                across = []
                for t in range(q * tiles // fold, (q + 1) * tiles // fold):
                    at = t * band + g * rows
                    across.append(change[at:at + rows])
                pieces.append(jnp.concatenate(across, axis=1))
            change_ref[g] = jnp.concatenate(pieces, axis=0).astype(jnp.bfloat16)
        fetches[2].wait()

    whole = pl.BlockSpec(memory_space=pltpu.VMEM)
    share = tiles * band // sites
    return pl.pallas_call(
        body,
        in_specs=[pl.BlockSpec(memory_space=pl.ANY)] * 3 + [whole],
        out_specs=(whole,) * 4,
        out_shape=(
            jax.ShapeDtypeStruct((sites, share, 128), jnp.bfloat16),
            jax.ShapeDtypeStruct((groups, fold * rows, rows_all), jnp.bfloat16),
            jax.ShapeDtypeStruct((nx * rows, 128), jnp.float32),
            jax.ShapeDtypeStruct(held_tokens.shape, jnp.bfloat16),
        ),
        scratch_shapes=[pltpu.VMEM((tiles * band, 128), jnp.float32)] * 2
        + [pltpu.VMEM(terms.shape, terms.dtype), pltpu.VMEM(side.shape, side.dtype), pltpu.SemaphoreType.DMA((3,))],
        compiler_params=params(),
        name="raise_and_pick",
    )(terms, side, held_tokens, table)


def update(sent, held, table, copies):
    sites, high, lanes = sent.shape

    def body(sent_ref, held_ref, table_ref, out_ref):
        total = sent_ref[0].astype(jnp.float32)
        for s in range(1, sites):
            total = total + sent_ref[s].astype(jnp.float32)
        fresh = (held_ref[...] - step_size * exact_dot(total, table_ref[...])).astype(jnp.bfloat16)
        for c in range(copies):
            out_ref[c] = fresh

    return pl.pallas_call(
        body,
        out_shape=jax.ShapeDtypeStruct((copies, high, lanes), jnp.bfloat16),
        compiler_params=params(),
        name="update",
    )(sent, held, table)


def project(tokens, mine, other, change):
    groups, tok, part = tokens.shape
    tiles, nyh, share, _ = mine.shape
    rows_all = 2 * nyh * share
    extra = change.shape[1]

    def body(tok_ref, mine_ref, other_ref, change_ref, out_ref):
        first = lax.axis_index("core") == 0
        weight = []
        for t in range(tiles):
            bands = []
            for y in range(nyh):
                a, b = mine_ref[t, y], other_ref[t, y]
                bands += [jnp.where(first, a, b), jnp.where(first, b, a)]
            weight.append(jnp.concatenate(bands, axis=0))
        weight = jnp.concatenate(weight, axis=1)
        weight = weight.T
        for k in range(0, groups, 2):
            both = jnp.concatenate([tok_ref[k], tok_ref[k + 1]], axis=0)
            both = jnp.dot(both, weight, preferred_element_type=jnp.float32).astype(out_ref.dtype)
            out_ref[k, :tok, :] = both[:tok]
            out_ref[k + 1, :tok, :] = both[tok:]
        for k in range(groups):
            out_ref[k, tok:, :] = change_ref[k]

    return pl.pallas_call(
        body,
        out_shape=jax.ShapeDtypeStruct((groups, tok + extra, rows_all), jnp.bfloat16),
        compiler_params=params(),
        name="project",
    )(tokens, mine, other, change)


def finish(parts, momentum, tok):
    groups, high, rows_all = parts.shape
    rows, width = momentum.shape
    part = width // groups

    def body(parts_ref, mom_ref, scores_ref, out_ref):
        scores = parts_ref[0, :tok, :].astype(jnp.float32)
        for k in range(1, groups):
            scores = scores + parts_ref[k, :tok, :].astype(jnp.float32)
        scores_ref[...] = scores.astype(jnp.bfloat16)
        for g in range(groups):
            change = parts_ref[g, tok:, :].astype(jnp.float32)
            for q in range(part // rows_all):
                at = g * part + q * rows_all
                out_ref[:, at:at + rows_all] = (
                    momentum_decay * mom_ref[:, at:at + rows_all] + change[q * rows:(q + 1) * rows]
                )

    return pl.pallas_call(
        body,
        out_shape=(
            jax.ShapeDtypeStruct((tok, rows_all), jnp.bfloat16),
            jax.ShapeDtypeStruct((rows, width), jnp.float32),
        ),
        compiler_params=params(),
        name="finish",
    )(parts, momentum)


def exchange(value, axes):
    return lax.all_to_all(value, axes, 0, 0, tiled=True)


def shards(tokens, cotangent, weight, momentum, kept_index):
    nz, ncore, nyh, nyl, nx = (lax.axis_size(name) for name in ("z", "core", "yh", "yl", "x"))
    groups = nyl * nx
    sites = nz * ncore
    _, tok, width = tokens.shape
    rows_all = cotangent.shape[2]
    rows = weight.shape[0]
    part = width // groups
    band = rows_all // nyh
    table = jnp.asarray(pair_table())

    kept = kept_index.transpose(0, 1, 3, 2).reshape(sites, -1, width // 64)

    def reduce_rows(arrays):
        partial, held_tokens, side = gradient(arrays, tok, rows_all)
        return held_tokens, exchange(partial.reshape(nyh, band, part), "yh"), side

    def in_one(tokens, cotangent, momentum, weight, kept):
        return reduce_rows([exchange(pack_all(tokens, cotangent, momentum, weight, kept, groups), GROUP)])

    def in_two(tokens, cotangent, momentum, weight, kept):
        rest = exchange(pack_rest(cotangent, momentum, weight, kept, groups), GROUP)
        return reduce_rows([exchange(follow(split_tokens(tokens, groups), rest), GROUP), rest])

    held_tokens, terms, side = lax.cond(
        lax.axis_index("core") == 0, in_one, in_two, tokens[0], cotangent[0], momentum[0], weight, kept
    )
    sent, change, held, held_tokens = raise_and_pick(terms, side, held_tokens, table, sites, rows_all, nx)

    fresh = update(exchange(sent, SITE), held, table, nz * nyh)
    mine = exchange(fresh, ("z", "yh")).reshape(nz, nyh, band // ncore, 128)
    other = lax.ppermute(mine, "core", [(0, 1), (1, 0)])
    scores, moment_new = finish(exchange(project(held_tokens, mine, other, change), GROUP), momentum[0], tok)
    return (scores[None], moment_new[None])


def solution(mesh):
    grid = Mesh(mesh.devices.reshape(8, 2, 4, 2, 4), ("z", "core", "yh", "yl", "x"))
    placed = (
        P(SITE, DEV, None),
        P(SITE, DEV, None),
        P(DEV, None),
        P(SITE, DEV, None),
        P(None, DEV, None, None),
    )
    return jax.shard_map(
        shards,
        mesh=grid,
        in_specs=placed,
        out_specs=(P(SITE, DEV, None), P(SITE, DEV, None)),
        check_vma=False,
    )
```

```python
import numpy as np
import jax
import jax.numpy as jnp
from jax import lax
from jax.experimental import pallas as pl
from jax.experimental.pallas import tpu as pltpu
from jax.sharding import Mesh, PartitionSpec as P

momentum_decay = 0.999
step_size = 0.01
SITE = ("z", "core")
GROUP = ("yl", "x")
DEV = ("yh", "yl", "x")
MIB = 1024 * 1024
ACROSS = (((1,), (1,)), ((), ()))
LEAD = 32
SIDE = 16


def pair_table():
    freq = np.arange(64)[:, None]
    place = np.arange(64)[None, :]
    factor = np.where(freq == 0, np.sqrt(1.0 / 64.0), np.sqrt(2.0 / 64.0))
    one = factor * np.cos(np.pi * (2.0 * place + 1.0) * freq / 128.0)
    return np.kron(np.eye(2), one).astype(np.float32)


def exact_dot(a, b):
    return jnp.dot(a, b, precision=lax.Precision.HIGHEST, preferred_element_type=jnp.float32)


def iota(shape, axis):
    return lax.broadcasted_iota(jnp.int32, shape, axis)


def halves(a):
    high = a.astype(jnp.bfloat16)
    return high, (a - high.astype(jnp.float32)).astype(jnp.bfloat16)


def close_dot(a, b):
    (a_high, a_low), (b_high, b_low) = halves(a), halves(b)

    def dot(p, q):
        return jnp.dot(p, q, preferred_element_type=jnp.float32)

    return dot(a_high, b_high) + (dot(a_high, b_low) + dot(a_low, b_high))


def params(mib=16):
    return pltpu.CompilerParams(vmem_limit_bytes=mib * MIB)


def pack_all(tokens, cotangent, momentum, weight, kept, groups):
    tok, width = tokens.shape
    part = width // groups
    rows_all = cotangent.shape[1]
    rows = weight.shape[0]
    fold = part // rows_all
    extra = tok // fold
    _, entries, blocks = kept.shape
    below = extra + SIDE

    def body(tok_ref, cot_ref, mom_ref, weight_ref, kept_ref, out_ref, held_ref, cot_vmem, mom_vmem, weight_vmem,
             spots_ref, in_sem, part_sem, out_sem):
        fetches = [
            pltpu.make_async_copy(tok_ref.at[:, g * part:(g + 1) * part], held_ref.at[g, :tok, :], in_sem.at[g])
            for g in range(groups)
        ]
        sends = [pltpu.make_async_copy(held_ref.at[g], out_ref.at[g], out_sem.at[g]) for g in range(groups)]
        parts = [
            pltpu.make_async_copy(kept_ref.at[lax.axis_index(SITE)], spots_ref, part_sem.at[0]),
            pltpu.make_async_copy(cot_ref, cot_vmem, part_sem.at[1]),
            pltpu.make_async_copy(mom_ref, mom_vmem, part_sem.at[2]),
            pltpu.make_async_copy(weight_ref, weight_vmem, part_sem.at[3]),
        ]
        for fetch in parts + fetches:
            fetch.start()
        for fetch in parts:
            fetch.wait()
        z = lax.axis_index("z")
        spots = spots_ref[...].astype(jnp.float32).T
        unused = jnp.zeros((rows, part - 3 * 128), jnp.float32)
        span = part // 64
        for g in range(groups):
            for q in range(fold):
                held_ref[g, tok:tok + extra, q * rows_all:(q + 1) * rows_all] = cot_vmem[q * extra:(q + 1) * extra, :]
            tile = weight_vmem[:, pl.ds(pl.multiple_of(g * part + z * 128, 128), 128)].astype(jnp.float32)
            low = [spots[g * span + h * rows:g * span + (h + 1) * rows] for h in range(span // rows)]
            low = jnp.concatenate(low + [tile, unused], axis=1)
            side = jnp.concatenate([mom_vmem[:, g * part:(g + 1) * part], low], axis=0)
            held_ref[g, tok + extra:, :] = side.astype(jnp.bfloat16)
            fetches[g].wait()
            sends[g].start()
        for send in sends:
            send.wait()

    anywhere = pl.BlockSpec(memory_space=pl.ANY)
    return pl.pallas_call(
        body,
        in_specs=[anywhere] * 5,
        out_specs=anywhere,
        out_shape=jax.ShapeDtypeStruct((groups, tok + below, part), tokens.dtype),
        scratch_shapes=[
            pltpu.VMEM((groups, tok + below, part), tokens.dtype),
            pltpu.VMEM((tok, rows_all), cotangent.dtype),
            pltpu.VMEM((rows, width), jnp.float32),
            pltpu.VMEM((rows, width), weight.dtype),
            pltpu.VMEM((entries, blocks), jnp.int32),
            pltpu.SemaphoreType.DMA((groups,)),
            pltpu.SemaphoreType.DMA((4,)),
            pltpu.SemaphoreType.DMA((groups,)),
        ],
        compiler_params=params(62),
        name="pack_all",
    )(tokens, cotangent, momentum, weight, kept)


def split_tokens(tokens, groups):
    tok, width = tokens.shape
    part = width // groups

    def body(tok_ref, out_ref, sem):
        moves = [
            pltpu.make_async_copy(tok_ref.at[LEAD:, g * part:(g + 1) * part], out_ref.at[g], sem.at[g])
            for g in range(groups)
        ]
        for move in moves:
            move.start()
        for move in moves:
            move.wait()

    return pl.pallas_call(
        body,
        in_specs=[pl.BlockSpec(memory_space=pl.ANY)],
        out_specs=pl.BlockSpec(memory_space=pltpu.VMEM),
        out_shape=jax.ShapeDtypeStruct((groups, tok - LEAD, part), tokens.dtype),
        scratch_shapes=[pltpu.SemaphoreType.DMA((groups,))],
        compiler_params=params(),
        name="split_tokens",
    )(tokens)


def pack_rest(tokens, cotangent, momentum, weight, kept, groups):
    rows, width = momentum.shape
    part = width // groups
    tok, rows_all = cotangent.shape
    fold = part // rows_all
    extra = tok // fold
    _, entries, blocks = kept.shape

    def body(tok_ref, cot_ref, mom_ref, weight_ref, kept_ref, out_ref, cot_vmem, mom_vmem, weight_vmem, spots_ref, sem):
        parts = [
            pltpu.make_async_copy(kept_ref.at[lax.axis_index(SITE)], spots_ref, sem.at[0]),
            pltpu.make_async_copy(mom_ref, mom_vmem, sem.at[1]),
            pltpu.make_async_copy(weight_ref, weight_vmem, sem.at[2]),
            pltpu.make_async_copy(cot_ref, cot_vmem, sem.at[3]),
        ]
        leads = [
            pltpu.make_async_copy(
                tok_ref.at[:LEAD, g * part:(g + 1) * part], out_ref.at[g, :LEAD, :], sem.at[4 + g]
            )
            for g in range(groups)
        ]
        for fetch in parts + leads:
            fetch.start()
        for fetch in parts:
            fetch.wait()
        z = lax.axis_index("z")
        spots = spots_ref[...].astype(jnp.float32).T
        unused = jnp.zeros((rows, part - 3 * 128), jnp.float32)
        span = part // 64
        for g in range(groups):
            tile = weight_vmem[:, pl.ds(pl.multiple_of(g * part + z * 128, 128), 128)].astype(jnp.float32)
            low = [spots[g * span + h * rows:g * span + (h + 1) * rows] for h in range(span // rows)]
            low = jnp.concatenate(low + [tile, unused], axis=1)
            side = jnp.concatenate([mom_vmem[:, g * part:(g + 1) * part], low], axis=0)
            for q in range(fold):
                out_ref[g, LEAD:LEAD + extra, q * rows_all:(q + 1) * rows_all] = cot_vmem[q * extra:(q + 1) * extra, :]
            out_ref[g, LEAD + extra:, :] = side.astype(jnp.bfloat16)
        for lead in leads:
            lead.wait()

    anywhere = pl.BlockSpec(memory_space=pl.ANY)
    return pl.pallas_call(
        body,
        in_specs=[anywhere] * 5,
        out_specs=pl.BlockSpec(memory_space=pltpu.VMEM),
        out_shape=jax.ShapeDtypeStruct((groups, LEAD + extra + SIDE, part), jnp.bfloat16),
        scratch_shapes=[
            pltpu.VMEM((tok, rows_all), cotangent.dtype),
            pltpu.VMEM((rows, width), jnp.float32),
            pltpu.VMEM((rows, width), weight.dtype),
            pltpu.VMEM((entries, blocks), jnp.int32),
            pltpu.SemaphoreType.DMA((4 + groups,)),
        ],
        compiler_params=params(),
        name="pack_rest",
    )(tokens, cotangent, momentum, weight, kept)


def follow(value, before):
    def body(value_ref, before_ref, out_ref):
        pass

    anywhere = pl.BlockSpec(memory_space=pl.ANY)
    return pl.pallas_call(
        body,
        in_specs=[anywhere] * 2,
        out_specs=anywhere,
        out_shape=jax.ShapeDtypeStruct(value.shape, value.dtype),
        input_output_aliases={0: 0},
        compiler_params=params(),
        name="follow",
    )(value, before)


def gradient(arrays, tok, rows_all):
    groups, _, part = arrays[0].shape
    fold = part // rows_all
    extra = tok // fold
    cols = 256
    lead = 0 if len(arrays) == 1 else LEAD
    start = lead or tok

    def body(*refs):
        tok_ref, rest_ref = refs[0], refs[len(arrays) - 1]
        out_ref, tok_out, side_out, sem = refs[len(arrays):]
        moves = [
            pltpu.make_async_copy(tok_ref.at[:, :tok - lead, :], tok_out.at[:, lead:, :], sem.at[0]),
            pltpu.make_async_copy(rest_ref.at[:, start + extra:, :], side_out, sem.at[1]),
        ]
        if lead:
            moves.append(pltpu.make_async_copy(rest_ref.at[:, :lead, :], tok_out.at[:, :lead, :], sem.at[2]))
        for move in moves:
            move.start()
        left = jnp.concatenate(
            [
                rest_ref[k, start:start + extra, q * rows_all:(q + 1) * rows_all]
                for k in range(groups)
                for q in range(fold)
            ],
            axis=0,
        ).T
        for j in range(0, part, cols):
            right = []
            for k in range(groups):
                right += [rest_ref[k, :lead, j:j + cols]] * (lead > 0) + [tok_ref[k, :tok - lead, j:j + cols]]
            out_ref[:, j:j + cols] = jnp.dot(
                left, jnp.concatenate(right, axis=0), preferred_element_type=jnp.float32
            ).astype(out_ref.dtype)
        for move in moves:
            move.wait()

    whole = pl.BlockSpec(memory_space=pltpu.VMEM)
    anywhere = pl.BlockSpec(memory_space=pl.ANY)
    return pl.pallas_call(
        body,
        in_specs=[whole] * len(arrays),
        out_specs=(whole, anywhere, anywhere),
        out_shape=(
            jax.ShapeDtypeStruct((rows_all, part), jnp.bfloat16),
            jax.ShapeDtypeStruct((groups, tok, part), jnp.bfloat16),
            jax.ShapeDtypeStruct((groups, SIDE, part), jnp.bfloat16),
        ),
        scratch_shapes=[pltpu.SemaphoreType.DMA((3,))],
        compiler_params=params(),
        name="gradient",
    )(*arrays)


def raise_and_pick(terms, side, held_tokens, table, sites, rows_all, nx):
    nyh, band, part = terms.shape
    groups = side.shape[0]
    tiles = part // 128
    rows = band // groups
    fold = part // rows_all
    span = part // 64

    def body(terms_hbm, side_hbm, tok_hbm, table_ref, sent_ref, change_ref, held_ref, tok_ref, keep_ref, moment_ref,
             terms_ref, side_ref, sem):
        fetches = [
            pltpu.make_async_copy(side_hbm, side_ref, sem.at[0]),
            pltpu.make_async_copy(terms_hbm, terms_ref, sem.at[1]),
            pltpu.make_async_copy(tok_hbm, tok_ref, sem.at[2]),
        ]
        for fetch in fetches:
            fetch.start()
        core = lax.axis_index("core")
        fetches[0].wait()
        freq = iota((64, 128), 0).astype(jnp.float32)
        gather = iota((rows, 128), 0) == iota((rows, 128), 1) // (128 // rows)
        gather = jnp.where(gather, 1.0, 0.0).astype(jnp.bfloat16)
        for g in range(groups):
            side = side_ref[g].astype(jnp.float32)
            marks = []
            for b in range(span):
                line = side[rows + b % rows:rows + b % rows + 1, b // rows * 128:(b // rows + 1) * 128]
                marks.append(jnp.where(line == freq, 1.0, 0.0).astype(jnp.bfloat16))
            keep = lax.dot_general(
                gather, jnp.concatenate(marks, axis=0), ACROSS, preferred_element_type=jnp.float32
            )
            for t in range(tiles):
                at = t * band + g * rows
                keep_ref[at:at + rows, :] = keep[:, t * 128:(t + 1) * 128]
                moment_ref[at:at + rows, :] = momentum_decay * side[:rows, t * 128:(t + 1) * 128]
        for x in range(nx):
            side = side_ref[core * nx + x].astype(jnp.float32)
            held_ref[x * rows:(x + 1) * rows, :] = side[rows:2 * rows, span // rows * 128:(span // rows + 1) * 128]

        fetches[1].wait()
        grad = terms_ref[0].astype(jnp.float32)
        for k in range(1, nyh):
            grad = grad + terms_ref[k].astype(jnp.float32)
        grad = jnp.concatenate([grad[:, t * 128:(t + 1) * 128] for t in range(tiles)], axis=0)
        both = table_ref[...]
        picked = close_dot(moment_ref[...] + grad, both.T) * keep_ref[...]
        sent_ref[...] = picked.astype(jnp.bfloat16).reshape(sent_ref.shape)
        change = grad - close_dot(picked, both)
        for g in range(groups):
            pieces = []
            for q in range(fold):
                across = []
                for t in range(q * tiles // fold, (q + 1) * tiles // fold):
                    at = t * band + g * rows
                    across.append(change[at:at + rows])
                pieces.append(jnp.concatenate(across, axis=1))
            change_ref[g] = jnp.concatenate(pieces, axis=0).astype(jnp.bfloat16)
        fetches[2].wait()

    whole = pl.BlockSpec(memory_space=pltpu.VMEM)
    share = tiles * band // sites
    return pl.pallas_call(
        body,
        in_specs=[pl.BlockSpec(memory_space=pl.ANY)] * 3 + [whole],
        out_specs=(whole,) * 4,
        out_shape=(
            jax.ShapeDtypeStruct((sites, share, 128), jnp.bfloat16),
            jax.ShapeDtypeStruct((groups, fold * rows, rows_all), jnp.bfloat16),
            jax.ShapeDtypeStruct((nx * rows, 128), jnp.float32),
            jax.ShapeDtypeStruct(held_tokens.shape, jnp.bfloat16),
        ),
        scratch_shapes=[pltpu.VMEM((tiles * band, 128), jnp.float32)] * 2
        + [pltpu.VMEM(terms.shape, terms.dtype), pltpu.VMEM(side.shape, side.dtype), pltpu.SemaphoreType.DMA((3,))],
        compiler_params=params(),
        name="raise_and_pick",
    )(terms, side, held_tokens, table)


def update(sent, held, table, copies):
    sites, high, lanes = sent.shape

    def body(sent_ref, held_ref, table_ref, out_ref):
        total = sent_ref[0].astype(jnp.float32)
        for s in range(1, sites):
            total = total + sent_ref[s].astype(jnp.float32)
        fresh = (held_ref[...] - step_size * exact_dot(total, table_ref[...])).astype(jnp.bfloat16)
        for c in range(copies):
            out_ref[c] = fresh

    return pl.pallas_call(
        body,
        out_shape=jax.ShapeDtypeStruct((copies, high, lanes), jnp.bfloat16),
        compiler_params=params(),
        name="update",
    )(sent, held, table)


def project(tokens, mine, other, change):
    groups, tok, part = tokens.shape
    tiles, nyh, share, _ = mine.shape
    rows_all = 2 * nyh * share
    extra = change.shape[1]

    def body(tok_ref, mine_ref, other_ref, change_ref, out_ref):
        first = lax.axis_index("core") == 0
        weight = []
        for t in range(tiles):
            bands = []
            for y in range(nyh):
                a, b = mine_ref[t, y], other_ref[t, y]
                bands += [jnp.where(first, a, b), jnp.where(first, b, a)]
            weight.append(jnp.concatenate(bands, axis=0))
        weight = jnp.concatenate(weight, axis=1)
        weight = weight.T
        for k in range(0, groups, 2):
            both = jnp.concatenate([tok_ref[k], tok_ref[k + 1]], axis=0)
            both = jnp.dot(both, weight, preferred_element_type=jnp.float32).astype(out_ref.dtype)
            out_ref[k, :tok, :] = both[:tok]
            out_ref[k + 1, :tok, :] = both[tok:]
        for k in range(groups):
            out_ref[k, tok:, :] = change_ref[k]

    return pl.pallas_call(
        body,
        out_shape=jax.ShapeDtypeStruct((groups, tok + extra, rows_all), jnp.bfloat16),
        compiler_params=params(),
        name="project",
    )(tokens, mine, other, change)


def finish(parts, momentum, tok):
    groups, high, rows_all = parts.shape
    rows, width = momentum.shape
    part = width // groups

    def body(parts_ref, mom_ref, scores_ref, out_ref):
        scores = parts_ref[0, :tok, :].astype(jnp.float32)
        for k in range(1, groups):
            scores = scores + parts_ref[k, :tok, :].astype(jnp.float32)
        scores_ref[...] = scores.astype(jnp.bfloat16)
        for g in range(groups):
            change = parts_ref[g, tok:, :].astype(jnp.float32)
            for q in range(part // rows_all):
                at = g * part + q * rows_all
                out_ref[:, at:at + rows_all] = (
                    momentum_decay * mom_ref[:, at:at + rows_all] + change[q * rows:(q + 1) * rows]
                )

    return pl.pallas_call(
        body,
        out_shape=(
            jax.ShapeDtypeStruct((tok, rows_all), jnp.bfloat16),
            jax.ShapeDtypeStruct((rows, width), jnp.float32),
        ),
        compiler_params=params(),
        name="finish",
    )(parts, momentum)


def exchange(value, axes):
    return lax.all_to_all(value, axes, 0, 0, tiled=True)


def shards(tokens, cotangent, weight, momentum, kept_index):
    nz, ncore, nyh, nyl, nx = (lax.axis_size(name) for name in ("z", "core", "yh", "yl", "x"))
    groups = nyl * nx
    sites = nz * ncore
    _, tok, width = tokens.shape
    rows_all = cotangent.shape[2]
    rows = weight.shape[0]
    part = width // groups
    band = rows_all // nyh
    table = jnp.asarray(pair_table())

    kept = kept_index.transpose(0, 1, 3, 2).reshape(sites, -1, width // 64)

    def reduce_rows(arrays):
        partial, held_tokens, side = gradient(arrays, tok, rows_all)
        return held_tokens, exchange(partial.reshape(nyh, band, part), "yh"), side

    def in_one(tokens, cotangent, momentum, weight, kept):
        return reduce_rows([exchange(pack_all(tokens, cotangent, momentum, weight, kept, groups), GROUP)])

    def in_two(tokens, cotangent, momentum, weight, kept):
        rest = exchange(pack_rest(tokens, cotangent, momentum, weight, kept, groups), GROUP)
        return reduce_rows([exchange(follow(split_tokens(tokens, groups), rest), GROUP), rest])

    held_tokens, terms, side = lax.cond(
        lax.axis_index("core") == 0, in_one, in_two, tokens[0], cotangent[0], momentum[0], weight, kept
    )
    sent, change, held, held_tokens = raise_and_pick(terms, side, held_tokens, table, sites, rows_all, nx)

    fresh = update(exchange(sent, SITE), held, table, nz * nyh)
    mine = exchange(fresh, ("z", "yh")).reshape(nz, nyh, band // ncore, 128)
    other = lax.ppermute(mine, "core", [(0, 1), (1, 0)])
    scores, moment_new = finish(exchange(project(held_tokens, mine, other, change), GROUP), momentum[0], tok)
    return (scores[None], moment_new[None])


def solution(mesh):
    grid = Mesh(mesh.devices.reshape(8, 2, 4, 2, 4), ("z", "core", "yh", "yl", "x"))
    placed = (
        P(SITE, DEV, None),
        P(SITE, DEV, None),
        P(DEV, None),
        P(SITE, DEV, None),
        P(None, DEV, None, None),
    )
    return jax.shard_map(
        shards,
        mesh=grid,
        in_specs=placed,
        out_specs=(P(SITE, DEV, None), P(SITE, DEV, None)),
        check_vma=False,
    )
```

```python
import numpy as np
import jax
import jax.numpy as jnp
from jax import lax
from jax.experimental import pallas as pl
from jax.experimental.pallas import tpu as pltpu
from jax.sharding import Mesh, PartitionSpec as P

momentum_decay = 0.999
step_size = 0.01
SITE = ("z", "core")
GROUP = ("yl", "x")
DEV = ("yh", "yl", "x")
MIB = 1024 * 1024
ACROSS = (((1,), (1,)), ((), ()))
LEAD = 48
SIDE = 16


def pair_table():
    freq = np.arange(64)[:, None]
    place = np.arange(64)[None, :]
    factor = np.where(freq == 0, np.sqrt(1.0 / 64.0), np.sqrt(2.0 / 64.0))
    one = factor * np.cos(np.pi * (2.0 * place + 1.0) * freq / 128.0)
    return np.kron(np.eye(2), one).astype(np.float32)


def exact_dot(a, b):
    return jnp.dot(a, b, precision=lax.Precision.HIGHEST, preferred_element_type=jnp.float32)


def iota(shape, axis):
    return lax.broadcasted_iota(jnp.int32, shape, axis)


def halves(a):
    high = a.astype(jnp.bfloat16)
    return high, (a - high.astype(jnp.float32)).astype(jnp.bfloat16)


def close_dot(a, b):
    (a_high, a_low), (b_high, b_low) = halves(a), halves(b)

    def dot(p, q):
        return jnp.dot(p, q, preferred_element_type=jnp.float32)

    return dot(a_high, b_high) + (dot(a_high, b_low) + dot(a_low, b_high))


def params(mib=16):
    return pltpu.CompilerParams(vmem_limit_bytes=mib * MIB)


def pack_all(tokens, cotangent, momentum, weight, kept, groups):
    tok, width = tokens.shape
    part = width // groups
    rows_all = cotangent.shape[1]
    rows = weight.shape[0]
    fold = part // rows_all
    extra = tok // fold
    _, entries, blocks = kept.shape
    below = extra + SIDE

    def body(tok_ref, cot_ref, mom_ref, weight_ref, kept_ref, out_ref, held_ref, cot_vmem, mom_vmem, weight_vmem,
             spots_ref, in_sem, part_sem, out_sem):
        fetches = [
            pltpu.make_async_copy(tok_ref.at[:, g * part:(g + 1) * part], held_ref.at[g, :tok, :], in_sem.at[g])
            for g in range(groups)
        ]
        sends = [pltpu.make_async_copy(held_ref.at[g], out_ref.at[g], out_sem.at[g]) for g in range(groups)]
        parts = [
            pltpu.make_async_copy(kept_ref.at[lax.axis_index(SITE)], spots_ref, part_sem.at[0]),
            pltpu.make_async_copy(cot_ref, cot_vmem, part_sem.at[1]),
            pltpu.make_async_copy(mom_ref, mom_vmem, part_sem.at[2]),
            pltpu.make_async_copy(weight_ref, weight_vmem, part_sem.at[3]),
        ]
        for fetch in parts + fetches:
            fetch.start()
        for fetch in parts:
            fetch.wait()
        z = lax.axis_index("z")
        spots = spots_ref[...].astype(jnp.float32).T
        unused = jnp.zeros((rows, part - 3 * 128), jnp.float32)
        span = part // 64
        for g in range(groups):
            for q in range(fold):
                held_ref[g, tok:tok + extra, q * rows_all:(q + 1) * rows_all] = cot_vmem[q * extra:(q + 1) * extra, :]
            tile = weight_vmem[:, pl.ds(pl.multiple_of(g * part + z * 128, 128), 128)].astype(jnp.float32)
            low = [spots[g * span + h * rows:g * span + (h + 1) * rows] for h in range(span // rows)]
            low = jnp.concatenate(low + [tile, unused], axis=1)
            side = jnp.concatenate([mom_vmem[:, g * part:(g + 1) * part], low], axis=0)
            held_ref[g, tok + extra:, :] = side.astype(jnp.bfloat16)
            fetches[g].wait()
            sends[g].start()
        for send in sends:
            send.wait()

    anywhere = pl.BlockSpec(memory_space=pl.ANY)
    return pl.pallas_call(
        body,
        in_specs=[anywhere] * 5,
        out_specs=anywhere,
        out_shape=jax.ShapeDtypeStruct((groups, tok + below, part), tokens.dtype),
        scratch_shapes=[
            pltpu.VMEM((groups, tok + below, part), tokens.dtype),
            pltpu.VMEM((tok, rows_all), cotangent.dtype),
            pltpu.VMEM((rows, width), jnp.float32),
            pltpu.VMEM((rows, width), weight.dtype),
            pltpu.VMEM((entries, blocks), jnp.int32),
            pltpu.SemaphoreType.DMA((groups,)),
            pltpu.SemaphoreType.DMA((4,)),
            pltpu.SemaphoreType.DMA((groups,)),
        ],
        compiler_params=params(62),
        name="pack_all",
    )(tokens, cotangent, momentum, weight, kept)


def split_tokens(tokens, groups):
    tok, width = tokens.shape
    part = width // groups

    def body(tok_ref, out_ref, sem):
        moves = [
            pltpu.make_async_copy(tok_ref.at[LEAD:, g * part:(g + 1) * part], out_ref.at[g], sem.at[g])
            for g in range(groups)
        ]
        for move in moves:
            move.start()
        for move in moves:
            move.wait()

    return pl.pallas_call(
        body,
        in_specs=[pl.BlockSpec(memory_space=pl.ANY)],
        out_specs=pl.BlockSpec(memory_space=pltpu.VMEM),
        out_shape=jax.ShapeDtypeStruct((groups, tok - LEAD, part), tokens.dtype),
        scratch_shapes=[pltpu.SemaphoreType.DMA((groups,))],
        compiler_params=params(),
        name="split_tokens",
    )(tokens)


def pack_rest(tokens, cotangent, momentum, weight, kept, groups):
    rows, width = momentum.shape
    part = width // groups
    tok, rows_all = cotangent.shape
    fold = part // rows_all
    extra = tok // fold
    _, entries, blocks = kept.shape

    def body(tok_ref, cot_ref, mom_ref, weight_ref, kept_ref, out_ref, cot_vmem, mom_vmem, weight_vmem, spots_ref, sem):
        parts = [
            pltpu.make_async_copy(kept_ref.at[lax.axis_index(SITE)], spots_ref, sem.at[0]),
            pltpu.make_async_copy(mom_ref, mom_vmem, sem.at[1]),
            pltpu.make_async_copy(weight_ref, weight_vmem, sem.at[2]),
            pltpu.make_async_copy(cot_ref, cot_vmem, sem.at[3]),
        ]
        leads = [
            pltpu.make_async_copy(
                tok_ref.at[:LEAD, g * part:(g + 1) * part], out_ref.at[g, :LEAD, :], sem.at[4 + g]
            )
            for g in range(groups)
        ]
        for fetch in parts + leads:
            fetch.start()
        for fetch in parts:
            fetch.wait()
        z = lax.axis_index("z")
        spots = spots_ref[...].astype(jnp.float32).T
        unused = jnp.zeros((rows, part - 3 * 128), jnp.float32)
        span = part // 64
        for g in range(groups):
            tile = weight_vmem[:, pl.ds(pl.multiple_of(g * part + z * 128, 128), 128)].astype(jnp.float32)
            low = [spots[g * span + h * rows:g * span + (h + 1) * rows] for h in range(span // rows)]
            low = jnp.concatenate(low + [tile, unused], axis=1)
            side = jnp.concatenate([mom_vmem[:, g * part:(g + 1) * part], low], axis=0)
            for q in range(fold):
                out_ref[g, LEAD:LEAD + extra, q * rows_all:(q + 1) * rows_all] = cot_vmem[q * extra:(q + 1) * extra, :]
            out_ref[g, LEAD + extra:, :] = side.astype(jnp.bfloat16)
        for lead in leads:
            lead.wait()

    anywhere = pl.BlockSpec(memory_space=pl.ANY)
    return pl.pallas_call(
        body,
        in_specs=[anywhere] * 5,
        out_specs=pl.BlockSpec(memory_space=pltpu.VMEM),
        out_shape=jax.ShapeDtypeStruct((groups, LEAD + extra + SIDE, part), jnp.bfloat16),
        scratch_shapes=[
            pltpu.VMEM((tok, rows_all), cotangent.dtype),
            pltpu.VMEM((rows, width), jnp.float32),
            pltpu.VMEM((rows, width), weight.dtype),
            pltpu.VMEM((entries, blocks), jnp.int32),
            pltpu.SemaphoreType.DMA((4 + groups,)),
        ],
        compiler_params=params(),
        name="pack_rest",
    )(tokens, cotangent, momentum, weight, kept)


def follow(value, before):
    def body(value_ref, before_ref, out_ref):
        pass

    anywhere = pl.BlockSpec(memory_space=pl.ANY)
    return pl.pallas_call(
        body,
        in_specs=[anywhere] * 2,
        out_specs=anywhere,
        out_shape=jax.ShapeDtypeStruct(value.shape, value.dtype),
        input_output_aliases={0: 0},
        compiler_params=params(),
        name="follow",
    )(value, before)


def gradient(arrays, tok, rows_all):
    groups, _, part = arrays[0].shape
    fold = part // rows_all
    extra = tok // fold
    cols = 256
    lead = 0 if len(arrays) == 1 else LEAD
    start = lead or tok

    def body(*refs):
        tok_ref, rest_ref = refs[0], refs[len(arrays) - 1]
        out_ref, tok_out, side_out, sem = refs[len(arrays):]
        moves = [
            pltpu.make_async_copy(tok_ref.at[:, :tok - lead, :], tok_out.at[:, lead:, :], sem.at[0]),
            pltpu.make_async_copy(rest_ref.at[:, start + extra:, :], side_out, sem.at[1]),
        ]
        if lead:
            moves.append(pltpu.make_async_copy(rest_ref.at[:, :lead, :], tok_out.at[:, :lead, :], sem.at[2]))
        for move in moves:
            move.start()
        left = jnp.concatenate(
            [
                rest_ref[k, start:start + extra, q * rows_all:(q + 1) * rows_all]
                for k in range(groups)
                for q in range(fold)
            ],
            axis=0,
        ).T
        for j in range(0, part, cols):
            right = []
            for k in range(groups):
                right += [rest_ref[k, :lead, j:j + cols]] * (lead > 0) + [tok_ref[k, :tok - lead, j:j + cols]]
            out_ref[:, j:j + cols] = jnp.dot(
                left, jnp.concatenate(right, axis=0), preferred_element_type=jnp.float32
            ).astype(out_ref.dtype)
        for move in moves:
            move.wait()

    whole = pl.BlockSpec(memory_space=pltpu.VMEM)
    anywhere = pl.BlockSpec(memory_space=pl.ANY)
    return pl.pallas_call(
        body,
        in_specs=[whole] * len(arrays),
        out_specs=(whole, anywhere, anywhere),
        out_shape=(
            jax.ShapeDtypeStruct((rows_all, part), jnp.bfloat16),
            jax.ShapeDtypeStruct((groups, tok, part), jnp.bfloat16),
            jax.ShapeDtypeStruct((groups, SIDE, part), jnp.bfloat16),
        ),
        scratch_shapes=[pltpu.SemaphoreType.DMA((3,))],
        compiler_params=params(),
        name="gradient",
    )(*arrays)


def raise_and_pick(terms, side, held_tokens, table, sites, rows_all, nx):
    nyh, band, part = terms.shape
    groups = side.shape[0]
    tiles = part // 128
    rows = band // groups
    fold = part // rows_all
    span = part // 64

    def body(terms_hbm, side_hbm, tok_hbm, table_ref, sent_ref, change_ref, held_ref, tok_ref, keep_ref, moment_ref,
             terms_ref, side_ref, sem):
        fetches = [
            pltpu.make_async_copy(side_hbm, side_ref, sem.at[0]),
            pltpu.make_async_copy(terms_hbm, terms_ref, sem.at[1]),
            pltpu.make_async_copy(tok_hbm, tok_ref, sem.at[2]),
        ]
        for fetch in fetches:
            fetch.start()
        core = lax.axis_index("core")
        fetches[0].wait()
        freq = iota((64, 128), 0).astype(jnp.float32)
        gather = iota((rows, 128), 0) == iota((rows, 128), 1) // (128 // rows)
        gather = jnp.where(gather, 1.0, 0.0).astype(jnp.bfloat16)
        for g in range(groups):
            side = side_ref[g].astype(jnp.float32)
            marks = []
            for b in range(span):
                line = side[rows + b % rows:rows + b % rows + 1, b // rows * 128:(b // rows + 1) * 128]
                marks.append(jnp.where(line == freq, 1.0, 0.0).astype(jnp.bfloat16))
            keep = lax.dot_general(
                gather, jnp.concatenate(marks, axis=0), ACROSS, preferred_element_type=jnp.float32
            )
            for t in range(tiles):
                at = t * band + g * rows
                keep_ref[at:at + rows, :] = keep[:, t * 128:(t + 1) * 128]
                moment_ref[at:at + rows, :] = momentum_decay * side[:rows, t * 128:(t + 1) * 128]
        for x in range(nx):
            side = side_ref[core * nx + x].astype(jnp.float32)
            held_ref[x * rows:(x + 1) * rows, :] = side[rows:2 * rows, span // rows * 128:(span // rows + 1) * 128]

        fetches[1].wait()
        grad = terms_ref[0].astype(jnp.float32)
        for k in range(1, nyh):
            grad = grad + terms_ref[k].astype(jnp.float32)
        grad = jnp.concatenate([grad[:, t * 128:(t + 1) * 128] for t in range(tiles)], axis=0)
        both = table_ref[...]
        picked = close_dot(moment_ref[...] + grad, both.T) * keep_ref[...]
        sent_ref[...] = picked.astype(jnp.bfloat16).reshape(sent_ref.shape)
        change = grad - close_dot(picked, both)
        for g in range(groups):
            pieces = []
            for q in range(fold):
                across = []
                for t in range(q * tiles // fold, (q + 1) * tiles // fold):
                    at = t * band + g * rows
                    across.append(change[at:at + rows])
                pieces.append(jnp.concatenate(across, axis=1))
            change_ref[g] = jnp.concatenate(pieces, axis=0).astype(jnp.bfloat16)
        fetches[2].wait()

    whole = pl.BlockSpec(memory_space=pltpu.VMEM)
    share = tiles * band // sites
    return pl.pallas_call(
        body,
        in_specs=[pl.BlockSpec(memory_space=pl.ANY)] * 3 + [whole],
        out_specs=(whole,) * 4,
        out_shape=(
            jax.ShapeDtypeStruct((sites, share, 128), jnp.bfloat16),
            jax.ShapeDtypeStruct((groups, fold * rows, rows_all), jnp.bfloat16),
            jax.ShapeDtypeStruct((nx * rows, 128), jnp.float32),
            jax.ShapeDtypeStruct(held_tokens.shape, jnp.bfloat16),
        ),
        scratch_shapes=[pltpu.VMEM((tiles * band, 128), jnp.float32)] * 2
        + [pltpu.VMEM(terms.shape, terms.dtype), pltpu.VMEM(side.shape, side.dtype), pltpu.SemaphoreType.DMA((3,))],
        compiler_params=params(),
        name="raise_and_pick",
    )(terms, side, held_tokens, table)


def update(sent, held, table, copies):
    sites, high, lanes = sent.shape

    def body(sent_ref, held_ref, table_ref, out_ref):
        total = sent_ref[0].astype(jnp.float32)
        for s in range(1, sites):
            total = total + sent_ref[s].astype(jnp.float32)
        fresh = (held_ref[...] - step_size * exact_dot(total, table_ref[...])).astype(jnp.bfloat16)
        for c in range(copies):
            out_ref[c] = fresh

    return pl.pallas_call(
        body,
        out_shape=jax.ShapeDtypeStruct((copies, high, lanes), jnp.bfloat16),
        compiler_params=params(),
        name="update",
    )(sent, held, table)


def project(tokens, mine, other, change):
    groups, tok, part = tokens.shape
    tiles, nyh, share, _ = mine.shape
    rows_all = 2 * nyh * share
    extra = change.shape[1]

    def body(tok_ref, mine_ref, other_ref, change_ref, out_ref):
        first = lax.axis_index("core") == 0
        weight = []
        for t in range(tiles):
            bands = []
            for y in range(nyh):
                a, b = mine_ref[t, y], other_ref[t, y]
                bands += [jnp.where(first, a, b), jnp.where(first, b, a)]
            weight.append(jnp.concatenate(bands, axis=0))
        weight = jnp.concatenate(weight, axis=1)
        weight = weight.T
        for k in range(0, groups, 2):
            both = jnp.concatenate([tok_ref[k], tok_ref[k + 1]], axis=0)
            both = jnp.dot(both, weight, preferred_element_type=jnp.float32).astype(out_ref.dtype)
            out_ref[k, :tok, :] = both[:tok]
            out_ref[k + 1, :tok, :] = both[tok:]
        for k in range(groups):
            out_ref[k, tok:, :] = change_ref[k]

    return pl.pallas_call(
        body,
        out_shape=jax.ShapeDtypeStruct((groups, tok + extra, rows_all), jnp.bfloat16),
        compiler_params=params(),
        name="project",
    )(tokens, mine, other, change)


def finish(parts, momentum, tok):
    groups, high, rows_all = parts.shape
    rows, width = momentum.shape
    part = width // groups

    def body(parts_ref, mom_ref, scores_ref, out_ref):
        scores = parts_ref[0, :tok, :].astype(jnp.float32)
        for k in range(1, groups):
            scores = scores + parts_ref[k, :tok, :].astype(jnp.float32)
        scores_ref[...] = scores.astype(jnp.bfloat16)
        for g in range(groups):
            change = parts_ref[g, tok:, :].astype(jnp.float32)
            for q in range(part // rows_all):
                at = g * part + q * rows_all
                out_ref[:, at:at + rows_all] = (
                    momentum_decay * mom_ref[:, at:at + rows_all] + change[q * rows:(q + 1) * rows]
                )

    return pl.pallas_call(
        body,
        out_shape=(
            jax.ShapeDtypeStruct((tok, rows_all), jnp.bfloat16),
            jax.ShapeDtypeStruct((rows, width), jnp.float32),
        ),
        compiler_params=params(),
        name="finish",
    )(parts, momentum)


def exchange(value, axes):
    return lax.all_to_all(value, axes, 0, 0, tiled=True)


def shards(tokens, cotangent, weight, momentum, kept_index):
    nz, ncore, nyh, nyl, nx = (lax.axis_size(name) for name in ("z", "core", "yh", "yl", "x"))
    groups = nyl * nx
    sites = nz * ncore
    _, tok, width = tokens.shape
    rows_all = cotangent.shape[2]
    rows = weight.shape[0]
    part = width // groups
    band = rows_all // nyh
    table = jnp.asarray(pair_table())

    kept = kept_index.transpose(0, 1, 3, 2).reshape(sites, -1, width // 64)

    def reduce_rows(arrays):
        partial, held_tokens, side = gradient(arrays, tok, rows_all)
        return held_tokens, exchange(partial.reshape(nyh, band, part), "yh"), side

    def in_one(tokens, cotangent, momentum, weight, kept):
        return reduce_rows([exchange(pack_all(tokens, cotangent, momentum, weight, kept, groups), GROUP)])

    def in_two(tokens, cotangent, momentum, weight, kept):
        rest = exchange(pack_rest(tokens, cotangent, momentum, weight, kept, groups), GROUP)
        return reduce_rows([exchange(follow(split_tokens(tokens, groups), rest), GROUP), rest])

    held_tokens, terms, side = lax.cond(
        lax.axis_index("core") == 0, in_one, in_two, tokens[0], cotangent[0], momentum[0], weight, kept
    )
    sent, change, held, held_tokens = raise_and_pick(terms, side, held_tokens, table, sites, rows_all, nx)

    fresh = update(exchange(sent, SITE), held, table, nz * nyh)
    mine = exchange(fresh, ("z", "yh")).reshape(nz, nyh, band // ncore, 128)
    other = lax.ppermute(mine, "core", [(0, 1), (1, 0)])
    scores, moment_new = finish(exchange(project(held_tokens, mine, other, change), GROUP), momentum[0], tok)
    return (scores[None], moment_new[None])


def solution(mesh):
    grid = Mesh(mesh.devices.reshape(8, 2, 4, 2, 4), ("z", "core", "yh", "yl", "x"))
    placed = (
        P(SITE, DEV, None),
        P(SITE, DEV, None),
        P(DEV, None),
        P(SITE, DEV, None),
        P(None, DEV, None, None),
    )
    return jax.shard_map(
        shards,
        mesh=grid,
        in_specs=placed,
        out_specs=(P(SITE, DEV, None), P(SITE, DEV, None)),
        check_vma=False,
    )
```

```python
import numpy as np
import jax
import jax.numpy as jnp
from jax import lax
from jax.experimental import pallas as pl
from jax.experimental.pallas import tpu as pltpu
from jax.sharding import Mesh, PartitionSpec as P

momentum_decay = 0.999
step_size = 0.01
SITE = ("z", "core")
GROUP = ("yl", "x")
DEV = ("yh", "yl", "x")
MIB = 1024 * 1024
ACROSS = (((1,), (1,)), ((), ()))
LEAD = 16
SIDE = 16


def pair_table():
    freq = np.arange(64)[:, None]
    place = np.arange(64)[None, :]
    factor = np.where(freq == 0, np.sqrt(1.0 / 64.0), np.sqrt(2.0 / 64.0))
    one = factor * np.cos(np.pi * (2.0 * place + 1.0) * freq / 128.0)
    return np.kron(np.eye(2), one).astype(np.float32)


def exact_dot(a, b):
    return jnp.dot(a, b, precision=lax.Precision.HIGHEST, preferred_element_type=jnp.float32)


def iota(shape, axis):
    return lax.broadcasted_iota(jnp.int32, shape, axis)


def halves(a):
    high = a.astype(jnp.bfloat16)
    return high, (a - high.astype(jnp.float32)).astype(jnp.bfloat16)


def close_dot(a, b):
    (a_high, a_low), (b_high, b_low) = halves(a), halves(b)

    def dot(p, q):
        return jnp.dot(p, q, preferred_element_type=jnp.float32)

    return dot(a_high, b_high) + (dot(a_high, b_low) + dot(a_low, b_high))


def params(mib=16):
    return pltpu.CompilerParams(vmem_limit_bytes=mib * MIB)


def pack_all(tokens, cotangent, momentum, weight, kept, groups):
    tok, width = tokens.shape
    part = width // groups
    rows_all = cotangent.shape[1]
    rows = weight.shape[0]
    fold = part // rows_all
    extra = tok // fold
    _, entries, blocks = kept.shape
    below = extra + SIDE

    def body(tok_ref, cot_ref, mom_ref, weight_ref, kept_ref, out_ref, held_ref, cot_vmem, mom_vmem, weight_vmem,
             spots_ref, in_sem, part_sem, out_sem):
        fetches = [
            pltpu.make_async_copy(tok_ref.at[:, g * part:(g + 1) * part], held_ref.at[g, :tok, :], in_sem.at[g])
            for g in range(groups)
        ]
        sends = [pltpu.make_async_copy(held_ref.at[g], out_ref.at[g], out_sem.at[g]) for g in range(groups)]
        parts = [
            pltpu.make_async_copy(kept_ref.at[lax.axis_index(SITE)], spots_ref, part_sem.at[0]),
            pltpu.make_async_copy(cot_ref, cot_vmem, part_sem.at[1]),
            pltpu.make_async_copy(mom_ref, mom_vmem, part_sem.at[2]),
            pltpu.make_async_copy(weight_ref, weight_vmem, part_sem.at[3]),
        ]
        for fetch in parts + fetches:
            fetch.start()
        for fetch in parts:
            fetch.wait()
        z = lax.axis_index("z")
        spots = spots_ref[...].astype(jnp.float32).T
        unused = jnp.zeros((rows, part - 3 * 128), jnp.float32)
        span = part // 64
        for g in range(groups):
            for q in range(fold):
                held_ref[g, tok:tok + extra, q * rows_all:(q + 1) * rows_all] = cot_vmem[q * extra:(q + 1) * extra, :]
            tile = weight_vmem[:, pl.ds(pl.multiple_of(g * part + z * 128, 128), 128)].astype(jnp.float32)
            low = [spots[g * span + h * rows:g * span + (h + 1) * rows] for h in range(span // rows)]
            low = jnp.concatenate(low + [tile, unused], axis=1)
            side = jnp.concatenate([mom_vmem[:, g * part:(g + 1) * part], low], axis=0)
            held_ref[g, tok + extra:, :] = side.astype(jnp.bfloat16)
            fetches[g].wait()
            sends[g].start()
        for send in sends:
            send.wait()

    anywhere = pl.BlockSpec(memory_space=pl.ANY)
    return pl.pallas_call(
        body,
        in_specs=[anywhere] * 5,
        out_specs=anywhere,
        out_shape=jax.ShapeDtypeStruct((groups, tok + below, part), tokens.dtype),
        scratch_shapes=[
            pltpu.VMEM((groups, tok + below, part), tokens.dtype),
            pltpu.VMEM((tok, rows_all), cotangent.dtype),
            pltpu.VMEM((rows, width), jnp.float32),
            pltpu.VMEM((rows, width), weight.dtype),
            pltpu.VMEM((entries, blocks), jnp.int32),
            pltpu.SemaphoreType.DMA((groups,)),
            pltpu.SemaphoreType.DMA((4,)),
            pltpu.SemaphoreType.DMA((groups,)),
        ],
        compiler_params=params(62),
        name="pack_all",
    )(tokens, cotangent, momentum, weight, kept)


def split_tokens(tokens, groups):
    tok, width = tokens.shape
    part = width // groups

    def body(tok_ref, out_ref, sem):
        moves = [
            pltpu.make_async_copy(tok_ref.at[LEAD:, g * part:(g + 1) * part], out_ref.at[g], sem.at[g])
            for g in range(groups)
        ]
        for move in moves:
            move.start()
        for move in moves:
            move.wait()

    return pl.pallas_call(
        body,
        in_specs=[pl.BlockSpec(memory_space=pl.ANY)],
        out_specs=pl.BlockSpec(memory_space=pltpu.VMEM),
        out_shape=jax.ShapeDtypeStruct((groups, tok - LEAD, part), tokens.dtype),
        scratch_shapes=[pltpu.SemaphoreType.DMA((groups,))],
        compiler_params=params(),
        name="split_tokens",
    )(tokens)


def pack_rest(tokens, cotangent, momentum, weight, kept, groups):
    rows, width = momentum.shape
    part = width // groups
    tok, rows_all = cotangent.shape
    fold = part // rows_all
    extra = tok // fold
    _, entries, blocks = kept.shape

    def body(tok_ref, cot_ref, mom_ref, weight_ref, kept_ref, out_ref, cot_vmem, mom_vmem, weight_vmem, spots_ref, sem):
        parts = [
            pltpu.make_async_copy(kept_ref.at[lax.axis_index(SITE)], spots_ref, sem.at[0]),
            pltpu.make_async_copy(mom_ref, mom_vmem, sem.at[1]),
            pltpu.make_async_copy(weight_ref, weight_vmem, sem.at[2]),
            pltpu.make_async_copy(cot_ref, cot_vmem, sem.at[3]),
        ]
        leads = [
            pltpu.make_async_copy(
                tok_ref.at[:LEAD, g * part:(g + 1) * part], out_ref.at[g, :LEAD, :], sem.at[4 + g]
            )
            for g in range(groups)
        ]
        for fetch in parts + leads:
            fetch.start()
        for fetch in parts:
            fetch.wait()
        z = lax.axis_index("z")
        spots = spots_ref[...].astype(jnp.float32).T
        unused = jnp.zeros((rows, part - 3 * 128), jnp.float32)
        span = part // 64
        for g in range(groups):
            tile = weight_vmem[:, pl.ds(pl.multiple_of(g * part + z * 128, 128), 128)].astype(jnp.float32)
            low = [spots[g * span + h * rows:g * span + (h + 1) * rows] for h in range(span // rows)]
            low = jnp.concatenate(low + [tile, unused], axis=1)
            side = jnp.concatenate([mom_vmem[:, g * part:(g + 1) * part], low], axis=0)
            for q in range(fold):
                out_ref[g, LEAD:LEAD + extra, q * rows_all:(q + 1) * rows_all] = cot_vmem[q * extra:(q + 1) * extra, :]
            out_ref[g, LEAD + extra:, :] = side.astype(jnp.bfloat16)
        for lead in leads:
            lead.wait()

    anywhere = pl.BlockSpec(memory_space=pl.ANY)
    return pl.pallas_call(
        body,
        in_specs=[anywhere] * 5,
        out_specs=pl.BlockSpec(memory_space=pltpu.VMEM),
        out_shape=jax.ShapeDtypeStruct((groups, LEAD + extra + SIDE, part), jnp.bfloat16),
        scratch_shapes=[
            pltpu.VMEM((tok, rows_all), cotangent.dtype),
            pltpu.VMEM((rows, width), jnp.float32),
            pltpu.VMEM((rows, width), weight.dtype),
            pltpu.VMEM((entries, blocks), jnp.int32),
            pltpu.SemaphoreType.DMA((4 + groups,)),
        ],
        compiler_params=params(),
        name="pack_rest",
    )(tokens, cotangent, momentum, weight, kept)


def follow(value, before):
    def body(value_ref, before_ref, out_ref):
        pass

    anywhere = pl.BlockSpec(memory_space=pl.ANY)
    return pl.pallas_call(
        body,
        in_specs=[anywhere] * 2,
        out_specs=anywhere,
        out_shape=jax.ShapeDtypeStruct(value.shape, value.dtype),
        input_output_aliases={0: 0},
        compiler_params=params(),
        name="follow",
    )(value, before)


def gradient(arrays, tok, rows_all):
    groups, _, part = arrays[0].shape
    fold = part // rows_all
    extra = tok // fold
    cols = 256
    lead = 0 if len(arrays) == 1 else LEAD
    start = lead or tok

    def body(*refs):
        tok_ref, rest_ref = refs[0], refs[len(arrays) - 1]
        out_ref, tok_out, side_out, sem = refs[len(arrays):]
        moves = [
            pltpu.make_async_copy(tok_ref.at[:, :tok - lead, :], tok_out.at[:, lead:, :], sem.at[0]),
            pltpu.make_async_copy(rest_ref.at[:, start + extra:, :], side_out, sem.at[1]),
        ]
        if lead:
            moves.append(pltpu.make_async_copy(rest_ref.at[:, :lead, :], tok_out.at[:, :lead, :], sem.at[2]))
        for move in moves:
            move.start()
        left = jnp.concatenate(
            [
                rest_ref[k, start:start + extra, q * rows_all:(q + 1) * rows_all]
                for k in range(groups)
                for q in range(fold)
            ],
            axis=0,
        ).T
        for j in range(0, part, cols):
            right = []
            for k in range(groups):
                right += [rest_ref[k, :lead, j:j + cols]] * (lead > 0) + [tok_ref[k, :tok - lead, j:j + cols]]
            out_ref[:, j:j + cols] = jnp.dot(
                left, jnp.concatenate(right, axis=0), preferred_element_type=jnp.float32
            ).astype(out_ref.dtype)
        for move in moves:
            move.wait()

    whole = pl.BlockSpec(memory_space=pltpu.VMEM)
    anywhere = pl.BlockSpec(memory_space=pl.ANY)
    return pl.pallas_call(
        body,
        in_specs=[whole] * len(arrays),
        out_specs=(whole, anywhere, anywhere),
        out_shape=(
            jax.ShapeDtypeStruct((rows_all, part), jnp.bfloat16),
            jax.ShapeDtypeStruct((groups, tok, part), jnp.bfloat16),
            jax.ShapeDtypeStruct((groups, SIDE, part), jnp.bfloat16),
        ),
        scratch_shapes=[pltpu.SemaphoreType.DMA((3,))],
        compiler_params=params(),
        name="gradient",
    )(*arrays)


def raise_and_pick(terms, side, held_tokens, table, sites, rows_all, nx):
    nyh, band, part = terms.shape
    groups = side.shape[0]
    tiles = part // 128
    rows = band // groups
    fold = part // rows_all
    span = part // 64

    def body(terms_hbm, side_hbm, tok_hbm, table_ref, sent_ref, change_ref, held_ref, tok_ref, keep_ref, moment_ref,
             terms_ref, side_ref, sem):
        fetches = [
            pltpu.make_async_copy(side_hbm, side_ref, sem.at[0]),
            pltpu.make_async_copy(terms_hbm, terms_ref, sem.at[1]),
            pltpu.make_async_copy(tok_hbm, tok_ref, sem.at[2]),
        ]
        for fetch in fetches:
            fetch.start()
        core = lax.axis_index("core")
        fetches[0].wait()
        freq = iota((64, 128), 0).astype(jnp.float32)
        gather = iota((rows, 128), 0) == iota((rows, 128), 1) // (128 // rows)
        gather = jnp.where(gather, 1.0, 0.0).astype(jnp.bfloat16)
        for g in range(groups):
            side = side_ref[g].astype(jnp.float32)
            marks = []
            for b in range(span):
                line = side[rows + b % rows:rows + b % rows + 1, b // rows * 128:(b // rows + 1) * 128]
                marks.append(jnp.where(line == freq, 1.0, 0.0).astype(jnp.bfloat16))
            keep = lax.dot_general(
                gather, jnp.concatenate(marks, axis=0), ACROSS, preferred_element_type=jnp.float32
            )
            for t in range(tiles):
                at = t * band + g * rows
                keep_ref[at:at + rows, :] = keep[:, t * 128:(t + 1) * 128]
                moment_ref[at:at + rows, :] = momentum_decay * side[:rows, t * 128:(t + 1) * 128]
        for x in range(nx):
            side = side_ref[core * nx + x].astype(jnp.float32)
            held_ref[x * rows:(x + 1) * rows, :] = side[rows:2 * rows, span // rows * 128:(span // rows + 1) * 128]

        fetches[1].wait()
        grad = terms_ref[0].astype(jnp.float32)
        for k in range(1, nyh):
            grad = grad + terms_ref[k].astype(jnp.float32)
        grad = jnp.concatenate([grad[:, t * 128:(t + 1) * 128] for t in range(tiles)], axis=0)
        both = table_ref[...]
        picked = close_dot(moment_ref[...] + grad, both.T) * keep_ref[...]
        sent_ref[...] = picked.astype(jnp.bfloat16).reshape(sent_ref.shape)
        change = grad - close_dot(picked, both)
        for g in range(groups):
            pieces = []
            for q in range(fold):
                across = []
                for t in range(q * tiles // fold, (q + 1) * tiles // fold):
                    at = t * band + g * rows
                    across.append(change[at:at + rows])
                pieces.append(jnp.concatenate(across, axis=1))
            change_ref[g] = jnp.concatenate(pieces, axis=0).astype(jnp.bfloat16)
        fetches[2].wait()

    whole = pl.BlockSpec(memory_space=pltpu.VMEM)
    share = tiles * band // sites
    return pl.pallas_call(
        body,
        in_specs=[pl.BlockSpec(memory_space=pl.ANY)] * 3 + [whole],
        out_specs=(whole,) * 4,
        out_shape=(
            jax.ShapeDtypeStruct((sites, share, 128), jnp.bfloat16),
            jax.ShapeDtypeStruct((groups, fold * rows, rows_all), jnp.bfloat16),
            jax.ShapeDtypeStruct((nx * rows, 128), jnp.float32),
            jax.ShapeDtypeStruct(held_tokens.shape, jnp.bfloat16),
        ),
        scratch_shapes=[pltpu.VMEM((tiles * band, 128), jnp.float32)] * 2
        + [pltpu.VMEM(terms.shape, terms.dtype), pltpu.VMEM(side.shape, side.dtype), pltpu.SemaphoreType.DMA((3,))],
        compiler_params=params(),
        name="raise_and_pick",
    )(terms, side, held_tokens, table)


def update(sent, held, table, copies):
    sites, high, lanes = sent.shape

    def body(sent_ref, held_ref, table_ref, out_ref):
        total = sent_ref[0].astype(jnp.float32)
        for s in range(1, sites):
            total = total + sent_ref[s].astype(jnp.float32)
        fresh = (held_ref[...] - step_size * exact_dot(total, table_ref[...])).astype(jnp.bfloat16)
        for c in range(copies):
            out_ref[c] = fresh

    return pl.pallas_call(
        body,
        out_shape=jax.ShapeDtypeStruct((copies, high, lanes), jnp.bfloat16),
        compiler_params=params(),
        name="update",
    )(sent, held, table)


def project(tokens, mine, other, change):
    groups, tok, part = tokens.shape
    tiles, nyh, share, _ = mine.shape
    rows_all = 2 * nyh * share
    extra = change.shape[1]

    def body(tok_ref, mine_ref, other_ref, change_ref, out_ref):
        first = lax.axis_index("core") == 0
        weight = []
        for t in range(tiles):
            bands = []
            for y in range(nyh):
                a, b = mine_ref[t, y], other_ref[t, y]
                bands += [jnp.where(first, a, b), jnp.where(first, b, a)]
            weight.append(jnp.concatenate(bands, axis=0))
        weight = jnp.concatenate(weight, axis=1)
        weight = weight.T
        for k in range(0, groups, 2):
            both = jnp.concatenate([tok_ref[k], tok_ref[k + 1]], axis=0)
            both = jnp.dot(both, weight, preferred_element_type=jnp.float32).astype(out_ref.dtype)
            out_ref[k, :tok, :] = both[:tok]
            out_ref[k + 1, :tok, :] = both[tok:]
        for k in range(groups):
            out_ref[k, tok:, :] = change_ref[k]

    return pl.pallas_call(
        body,
        out_shape=jax.ShapeDtypeStruct((groups, tok + extra, rows_all), jnp.bfloat16),
        compiler_params=params(),
        name="project",
    )(tokens, mine, other, change)


def finish(parts, momentum, tok):
    groups, high, rows_all = parts.shape
    rows, width = momentum.shape
    part = width // groups

    def body(parts_ref, mom_ref, scores_ref, out_ref):
        scores = parts_ref[0, :tok, :].astype(jnp.float32)
        for k in range(1, groups):
            scores = scores + parts_ref[k, :tok, :].astype(jnp.float32)
        scores_ref[...] = scores.astype(jnp.bfloat16)
        for g in range(groups):
            change = parts_ref[g, tok:, :].astype(jnp.float32)
            for q in range(part // rows_all):
                at = g * part + q * rows_all
                out_ref[:, at:at + rows_all] = (
                    momentum_decay * mom_ref[:, at:at + rows_all] + change[q * rows:(q + 1) * rows]
                )

    return pl.pallas_call(
        body,
        out_shape=(
            jax.ShapeDtypeStruct((tok, rows_all), jnp.bfloat16),
            jax.ShapeDtypeStruct((rows, width), jnp.float32),
        ),
        compiler_params=params(),
        name="finish",
    )(parts, momentum)


def exchange(value, axes):
    return lax.all_to_all(value, axes, 0, 0, tiled=True)


def shards(tokens, cotangent, weight, momentum, kept_index):
    nz, ncore, nyh, nyl, nx = (lax.axis_size(name) for name in ("z", "core", "yh", "yl", "x"))
    groups = nyl * nx
    sites = nz * ncore
    _, tok, width = tokens.shape
    rows_all = cotangent.shape[2]
    rows = weight.shape[0]
    part = width // groups
    band = rows_all // nyh
    table = jnp.asarray(pair_table())

    kept = kept_index.transpose(0, 1, 3, 2).reshape(sites, -1, width // 64)

    def reduce_rows(arrays):
        partial, held_tokens, side = gradient(arrays, tok, rows_all)
        return held_tokens, exchange(partial.reshape(nyh, band, part), "yh"), side

    def in_one(tokens, cotangent, momentum, weight, kept):
        return reduce_rows([exchange(pack_all(tokens, cotangent, momentum, weight, kept, groups), GROUP)])

    def in_two(tokens, cotangent, momentum, weight, kept):
        rest = exchange(pack_rest(tokens, cotangent, momentum, weight, kept, groups), GROUP)
        return reduce_rows([exchange(follow(split_tokens(tokens, groups), rest), GROUP), rest])

    held_tokens, terms, side = lax.cond(
        lax.axis_index("core") == 0, in_one, in_two, tokens[0], cotangent[0], momentum[0], weight, kept
    )
    sent, change, held, held_tokens = raise_and_pick(terms, side, held_tokens, table, sites, rows_all, nx)

    fresh = update(exchange(sent, SITE), held, table, nz * nyh)
    mine = exchange(fresh, ("z", "yh")).reshape(nz, nyh, band // ncore, 128)
    other = lax.ppermute(mine, "core", [(0, 1), (1, 0)])
    scores, moment_new = finish(exchange(project(held_tokens, mine, other, change), GROUP), momentum[0], tok)
    return (scores[None], moment_new[None])


def solution(mesh):
    grid = Mesh(mesh.devices.reshape(8, 2, 4, 2, 4), ("z", "core", "yh", "yl", "x"))
    placed = (
        P(SITE, DEV, None),
        P(SITE, DEV, None),
        P(DEV, None),
        P(SITE, DEV, None),
        P(None, DEV, None, None),
    )
    return jax.shard_map(
        shards,
        mesh=grid,
        in_specs=placed,
        out_specs=(P(SITE, DEV, None), P(SITE, DEV, None)),
        check_vma=False,
    )
```

```python
import numpy as np
import jax
import jax.numpy as jnp
from jax import lax
from jax.experimental import pallas as pl
from jax.experimental.pallas import tpu as pltpu
from jax.sharding import Mesh, PartitionSpec as P

momentum_decay = 0.999
step_size = 0.01
SITE = ("z", "core")
GROUP = ("yl", "x")
DEV = ("yh", "yl", "x")
MIB = 1024 * 1024
ACROSS = (((1,), (1,)), ((), ()))
LEAD = 32
SIDE = 16


def pair_table():
    freq = np.arange(64)[:, None]
    place = np.arange(64)[None, :]
    factor = np.where(freq == 0, np.sqrt(1.0 / 64.0), np.sqrt(2.0 / 64.0))
    one = factor * np.cos(np.pi * (2.0 * place + 1.0) * freq / 128.0)
    return np.kron(np.eye(2), one).astype(np.float32)


def exact_dot(a, b):
    return jnp.dot(a, b, precision=lax.Precision.HIGHEST, preferred_element_type=jnp.float32)


def iota(shape, axis):
    return lax.broadcasted_iota(jnp.int32, shape, axis)


def halves(a):
    high = a.astype(jnp.bfloat16)
    return high, (a - high.astype(jnp.float32)).astype(jnp.bfloat16)


def close_dot(a, b):
    (a_high, a_low), (b_high, b_low) = halves(a), halves(b)

    def dot(p, q):
        return jnp.dot(p, q, preferred_element_type=jnp.float32)

    return dot(a_high, b_high) + (dot(a_high, b_low) + dot(a_low, b_high))


def params(mib=16):
    return pltpu.CompilerParams(vmem_limit_bytes=mib * MIB)


def pack_all(tokens, cotangent, momentum, weight, kept, groups):
    tok, width = tokens.shape
    part = width // groups
    rows_all = cotangent.shape[1]
    rows = weight.shape[0]
    fold = part // rows_all
    extra = tok // fold
    _, entries, blocks = kept.shape
    below = extra + SIDE

    def body(tok_ref, cot_ref, mom_ref, weight_ref, kept_ref, out_ref, held_ref, cot_vmem, mom_vmem, weight_vmem,
             spots_ref, in_sem, part_sem, out_sem):
        fetches = [
            pltpu.make_async_copy(tok_ref.at[:, g * part:(g + 1) * part], held_ref.at[g, :tok, :], in_sem.at[g])
            for g in range(groups)
        ]
        sends = [pltpu.make_async_copy(held_ref.at[g], out_ref.at[g], out_sem.at[g]) for g in range(groups)]
        parts = [
            pltpu.make_async_copy(kept_ref.at[lax.axis_index(SITE)], spots_ref, part_sem.at[0]),
            pltpu.make_async_copy(cot_ref, cot_vmem, part_sem.at[1]),
            pltpu.make_async_copy(mom_ref, mom_vmem, part_sem.at[2]),
            pltpu.make_async_copy(weight_ref, weight_vmem, part_sem.at[3]),
        ]
        for fetch in parts + fetches:
            fetch.start()
        for fetch in parts:
            fetch.wait()
        z = lax.axis_index("z")
        spots = spots_ref[...].astype(jnp.float32).T
        unused = jnp.zeros((rows, part - 3 * 128), jnp.float32)
        span = part // 64
        for g in range(groups):
            for q in range(fold):
                held_ref[g, tok:tok + extra, q * rows_all:(q + 1) * rows_all] = cot_vmem[q * extra:(q + 1) * extra, :]
            tile = weight_vmem[:, pl.ds(pl.multiple_of(g * part + z * 128, 128), 128)].astype(jnp.float32)
            low = [spots[g * span + h * rows:g * span + (h + 1) * rows] for h in range(span // rows)]
            low = jnp.concatenate(low + [tile, unused], axis=1)
            side = jnp.concatenate([mom_vmem[:, g * part:(g + 1) * part], low], axis=0)
            held_ref[g, tok + extra:, :] = side.astype(jnp.bfloat16)
            fetches[g].wait()
            sends[g].start()
        for send in sends:
            send.wait()

    anywhere = pl.BlockSpec(memory_space=pl.ANY)
    return pl.pallas_call(
        body,
        in_specs=[anywhere] * 5,
        out_specs=anywhere,
        out_shape=jax.ShapeDtypeStruct((groups, tok + below, part), tokens.dtype),
        scratch_shapes=[
            pltpu.VMEM((groups, tok + below, part), tokens.dtype),
            pltpu.VMEM((tok, rows_all), cotangent.dtype),
            pltpu.VMEM((rows, width), jnp.float32),
            pltpu.VMEM((rows, width), weight.dtype),
            pltpu.VMEM((entries, blocks), jnp.int32),
            pltpu.SemaphoreType.DMA((groups,)),
            pltpu.SemaphoreType.DMA((4,)),
            pltpu.SemaphoreType.DMA((groups,)),
        ],
        compiler_params=params(62),
        name="pack_all",
    )(tokens, cotangent, momentum, weight, kept)


def split_tokens(tokens, groups):
    tok, width = tokens.shape
    part = width // groups

    def body(tok_ref, out_ref, sem):
        moves = [
            pltpu.make_async_copy(tok_ref.at[LEAD:, g * part:(g + 1) * part], out_ref.at[g], sem.at[g])
            for g in range(groups)
        ]
        for move in moves:
            move.start()
        for move in moves:
            move.wait()

    return pl.pallas_call(
        body,
        in_specs=[pl.BlockSpec(memory_space=pl.ANY)],
        out_specs=pl.BlockSpec(memory_space=pltpu.VMEM),
        out_shape=jax.ShapeDtypeStruct((groups, tok - LEAD, part), tokens.dtype),
        scratch_shapes=[pltpu.SemaphoreType.DMA((groups,))],
        compiler_params=params(),
        name="split_tokens",
    )(tokens)


def pack_rest(tokens, cotangent, momentum, weight, kept, groups):
    rows, width = momentum.shape
    part = width // groups
    tok, rows_all = cotangent.shape
    fold = part // rows_all
    extra = tok // fold
    _, entries, blocks = kept.shape

    def body(tok_ref, cot_ref, mom_ref, weight_ref, kept_ref, out_ref, cot_vmem, mom_vmem, weight_vmem, spots_ref, sem):
        parts = [
            pltpu.make_async_copy(kept_ref.at[lax.axis_index(SITE)], spots_ref, sem.at[0]),
            pltpu.make_async_copy(mom_ref, mom_vmem, sem.at[1]),
            pltpu.make_async_copy(weight_ref, weight_vmem, sem.at[2]),
            pltpu.make_async_copy(cot_ref, cot_vmem, sem.at[3]),
        ]
        leads = [
            pltpu.make_async_copy(
                tok_ref.at[:LEAD, g * part:(g + 1) * part], out_ref.at[g, :LEAD, :], sem.at[4 + g]
            )
            for g in range(groups)
        ]
        for fetch in parts + leads:
            fetch.start()
        for fetch in parts:
            fetch.wait()
        z = lax.axis_index("z")
        spots = spots_ref[...].astype(jnp.float32).T
        unused = jnp.zeros((rows, part - 3 * 128), jnp.float32)
        span = part // 64
        for g in range(groups):
            tile = weight_vmem[:, pl.ds(pl.multiple_of(g * part + z * 128, 128), 128)].astype(jnp.float32)
            low = [spots[g * span + h * rows:g * span + (h + 1) * rows] for h in range(span // rows)]
            low = jnp.concatenate(low + [tile, unused], axis=1)
            side = jnp.concatenate([mom_vmem[:, g * part:(g + 1) * part], low], axis=0)
            for q in range(fold):
                out_ref[g, LEAD:LEAD + extra, q * rows_all:(q + 1) * rows_all] = cot_vmem[q * extra:(q + 1) * extra, :]
            out_ref[g, LEAD + extra:, :] = side.astype(jnp.bfloat16)
        for lead in leads:
            lead.wait()

    anywhere = pl.BlockSpec(memory_space=pl.ANY)
    return pl.pallas_call(
        body,
        in_specs=[anywhere] * 5,
        out_specs=pl.BlockSpec(memory_space=pltpu.VMEM),
        out_shape=jax.ShapeDtypeStruct((groups, LEAD + extra + SIDE, part), jnp.bfloat16),
        scratch_shapes=[
            pltpu.VMEM((tok, rows_all), cotangent.dtype),
            pltpu.VMEM((rows, width), jnp.float32),
            pltpu.VMEM((rows, width), weight.dtype),
            pltpu.VMEM((entries, blocks), jnp.int32),
            pltpu.SemaphoreType.DMA((4 + groups,)),
        ],
        compiler_params=params(),
        name="pack_rest",
    )(tokens, cotangent, momentum, weight, kept)


def follow(value, before):
    def body(value_ref, before_ref, out_ref):
        pass

    anywhere = pl.BlockSpec(memory_space=pl.ANY)
    return pl.pallas_call(
        body,
        in_specs=[anywhere] * 2,
        out_specs=anywhere,
        out_shape=jax.ShapeDtypeStruct(value.shape, value.dtype),
        input_output_aliases={0: 0},
        compiler_params=params(),
        name="follow",
    )(value, before)


def gradient(arrays, tok, rows_all):
    groups, _, part = arrays[0].shape
    fold = part // rows_all
    extra = tok // fold
    cols = 256
    lead = 0 if len(arrays) == 1 else LEAD
    start = lead or tok

    def body(*refs):
        tok_ref, rest_ref = refs[0], refs[len(arrays) - 1]
        out_ref, tok_out, side_out, sem = refs[len(arrays):]
        moves = [
            pltpu.make_async_copy(tok_ref.at[:, :tok - lead, :], tok_out.at[:, lead:, :], sem.at[0]),
            pltpu.make_async_copy(rest_ref.at[:, start + extra:, :], side_out, sem.at[1]),
        ]
        if lead:
            moves.append(pltpu.make_async_copy(rest_ref.at[:, :lead, :], tok_out.at[:, :lead, :], sem.at[2]))
        for move in moves:
            move.start()
        left = jnp.concatenate(
            [
                rest_ref[k, start:start + extra, q * rows_all:(q + 1) * rows_all]
                for k in range(groups)
                for q in range(fold)
            ],
            axis=0,
        ).T
        for j in range(0, part, cols):
            right = []
            for k in range(groups):
                right += [rest_ref[k, :lead, j:j + cols]] * (lead > 0) + [tok_ref[k, :tok - lead, j:j + cols]]
            out_ref[:, j:j + cols] = jnp.dot(
                left, jnp.concatenate(right, axis=0), preferred_element_type=jnp.float32
            ).astype(out_ref.dtype)
        for move in moves:
            move.wait()

    whole = pl.BlockSpec(memory_space=pltpu.VMEM)
    anywhere = pl.BlockSpec(memory_space=pl.ANY)
    return pl.pallas_call(
        body,
        in_specs=[whole] * len(arrays),
        out_specs=(whole, anywhere, anywhere),
        out_shape=(
            jax.ShapeDtypeStruct((rows_all, part), jnp.bfloat16),
            jax.ShapeDtypeStruct((groups, tok, part), jnp.bfloat16),
            jax.ShapeDtypeStruct((groups, SIDE, part), jnp.bfloat16),
        ),
        scratch_shapes=[pltpu.SemaphoreType.DMA((3,))],
        compiler_params=params(),
        name="gradient",
    )(*arrays)


def raise_and_pick(terms, side, held_tokens, table, sites, rows_all, nx):
    nyh, band, part = terms.shape
    groups = side.shape[0]
    tiles = part // 128
    rows = band // groups
    fold = part // rows_all
    span = part // 64

    def body(terms_hbm, side_hbm, tok_hbm, table_ref, sent_ref, change_ref, held_ref, tok_ref, keep_ref, moment_ref,
             terms_ref, side_ref, sem):
        fetches = [
            pltpu.make_async_copy(side_hbm, side_ref, sem.at[0]),
            pltpu.make_async_copy(terms_hbm, terms_ref, sem.at[1]),
            pltpu.make_async_copy(tok_hbm, tok_ref, sem.at[2]),
        ]
        for fetch in fetches:
            fetch.start()
        core = lax.axis_index("core")
        fetches[0].wait()
        freq = iota((64, 128), 0).astype(jnp.float32)
        gather = iota((rows, 128), 0) == iota((rows, 128), 1) // (128 // rows)
        gather = jnp.where(gather, 1.0, 0.0).astype(jnp.bfloat16)
        for g in range(groups):
            side = side_ref[g].astype(jnp.float32)
            marks = []
            for b in range(span):
                line = side[rows + b % rows:rows + b % rows + 1, b // rows * 128:(b // rows + 1) * 128]
                marks.append(jnp.where(line == freq, 1.0, 0.0).astype(jnp.bfloat16))
            keep = lax.dot_general(
                gather, jnp.concatenate(marks, axis=0), ACROSS, preferred_element_type=jnp.float32
            )
            for t in range(tiles):
                at = t * band + g * rows
                keep_ref[at:at + rows, :] = keep[:, t * 128:(t + 1) * 128]
                moment_ref[at:at + rows, :] = momentum_decay * side[:rows, t * 128:(t + 1) * 128]
        for x in range(nx):
            side = side_ref[core * nx + x].astype(jnp.float32)
            held_ref[x * rows:(x + 1) * rows, :] = side[rows:2 * rows, span // rows * 128:(span // rows + 1) * 128]

        fetches[1].wait()
        grad = terms_ref[0].astype(jnp.float32)
        for k in range(1, nyh):
            grad = grad + terms_ref[k].astype(jnp.float32)
        grad = jnp.concatenate([grad[:, t * 128:(t + 1) * 128] for t in range(tiles)], axis=0)
        both = table_ref[...]
        picked = close_dot(moment_ref[...] + grad, both.T) * keep_ref[...]
        sent_ref[...] = picked.astype(jnp.bfloat16).reshape(sent_ref.shape)
        change = grad - close_dot(picked, both)
        for g in range(groups):
            pieces = []
            for q in range(fold):
                across = []
                for t in range(q * tiles // fold, (q + 1) * tiles // fold):
                    at = t * band + g * rows
                    across.append(change[at:at + rows])
                pieces.append(jnp.concatenate(across, axis=1))
            change_ref[g] = jnp.concatenate(pieces, axis=0).astype(jnp.bfloat16)
        fetches[2].wait()

    whole = pl.BlockSpec(memory_space=pltpu.VMEM)
    share = tiles * band // sites
    return pl.pallas_call(
        body,
        in_specs=[pl.BlockSpec(memory_space=pl.ANY)] * 3 + [whole],
        out_specs=(whole,) * 4,
        out_shape=(
            jax.ShapeDtypeStruct((sites, share, 128), jnp.bfloat16),
            jax.ShapeDtypeStruct((groups, fold * rows, rows_all), jnp.bfloat16),
            jax.ShapeDtypeStruct((nx * rows, 128), jnp.float32),
            jax.ShapeDtypeStruct(held_tokens.shape, jnp.bfloat16),
        ),
        scratch_shapes=[pltpu.VMEM((tiles * band, 128), jnp.float32)] * 2
        + [pltpu.VMEM(terms.shape, terms.dtype), pltpu.VMEM(side.shape, side.dtype), pltpu.SemaphoreType.DMA((3,))],
        compiler_params=params(),
        name="raise_and_pick",
    )(terms, side, held_tokens, table)


def update(sent, held, table, copies):
    sites, high, lanes = sent.shape

    def body(sent_ref, held_ref, table_ref, out_ref):
        total = sent_ref[0].astype(jnp.float32)
        for s in range(1, sites):
            total = total + sent_ref[s].astype(jnp.float32)
        fresh = (held_ref[...] - step_size * exact_dot(total, table_ref[...])).astype(jnp.bfloat16)
        for c in range(copies):
            out_ref[c] = fresh

    return pl.pallas_call(
        body,
        out_shape=jax.ShapeDtypeStruct((copies, high, lanes), jnp.bfloat16),
        compiler_params=params(),
        name="update",
    )(sent, held, table)


def project(tokens, mine, other, change):
    groups, tok, part = tokens.shape
    _, share, _ = mine.shape
    tiles = part // 128
    nyh = mine.shape[0] // tiles
    rows_all = 2 * nyh * share
    extra = change.shape[1]

    def body(tok_ref, mine_ref, other_ref, change_ref, out_ref):
        first = lax.axis_index("core") == 0
        weight = []
        for t in range(tiles):
            bands = []
            for y in range(nyh):
                at, other_at = t * nyh + y, y * tiles + t
                bands += [
                    jnp.where(first, mine_ref[at], other_ref[at]),
                    jnp.where(first, other_ref[other_at], mine_ref[other_at]),
                ]
            weight.append(jnp.concatenate(bands, axis=0))
        weight = jnp.concatenate(weight, axis=1)
        weight = weight.T
        for k in range(0, groups, 2):
            both = jnp.concatenate([tok_ref[k], tok_ref[k + 1]], axis=0)
            both = jnp.dot(both, weight, preferred_element_type=jnp.float32).astype(out_ref.dtype)
            out_ref[k, :tok, :] = both[:tok]
            out_ref[k + 1, :tok, :] = both[tok:]
        for k in range(groups):
            out_ref[k, tok:, :] = change_ref[k]

    return pl.pallas_call(
        body,
        out_shape=jax.ShapeDtypeStruct((groups, tok + extra, rows_all), jnp.bfloat16),
        compiler_params=params(),
        name="project",
    )(tokens, mine, other, change)


def finish(parts, momentum, tok):
    groups, high, rows_all = parts.shape
    rows, width = momentum.shape
    part = width // groups

    def body(parts_ref, mom_ref, scores_ref, out_ref):
        scores = parts_ref[0, :tok, :].astype(jnp.float32)
        for k in range(1, groups):
            scores = scores + parts_ref[k, :tok, :].astype(jnp.float32)
        scores_ref[...] = scores.astype(jnp.bfloat16)
        for g in range(groups):
            change = parts_ref[g, tok:, :].astype(jnp.float32)
            for q in range(part // rows_all):
                at = g * part + q * rows_all
                out_ref[:, at:at + rows_all] = (
                    momentum_decay * mom_ref[:, at:at + rows_all] + change[q * rows:(q + 1) * rows]
                )

    return pl.pallas_call(
        body,
        out_shape=(
            jax.ShapeDtypeStruct((tok, rows_all), jnp.bfloat16),
            jax.ShapeDtypeStruct((rows, width), jnp.float32),
        ),
        compiler_params=params(),
        name="finish",
    )(parts, momentum)


def exchange(value, axes):
    return lax.all_to_all(value, axes, 0, 0, tiled=True)


def shards(tokens, cotangent, weight, momentum, kept_index):
    nz, ncore, nyh, nyl, nx = (lax.axis_size(name) for name in ("z", "core", "yh", "yl", "x"))
    groups = nyl * nx
    sites = nz * ncore
    _, tok, width = tokens.shape
    rows_all = cotangent.shape[2]
    rows = weight.shape[0]
    part = width // groups
    band = rows_all // nyh
    table = jnp.asarray(pair_table())

    kept = kept_index.transpose(0, 1, 3, 2).reshape(sites, -1, width // 64)

    def reduce_rows(arrays):
        partial, held_tokens, side = gradient(arrays, tok, rows_all)
        return held_tokens, exchange(partial.reshape(nyh, band, part), "yh"), side

    def in_one(tokens, cotangent, momentum, weight, kept):
        return reduce_rows([exchange(pack_all(tokens, cotangent, momentum, weight, kept, groups), GROUP)])

    def in_two(tokens, cotangent, momentum, weight, kept):
        rest = exchange(pack_rest(tokens, cotangent, momentum, weight, kept, groups), GROUP)
        return reduce_rows([exchange(follow(split_tokens(tokens, groups), rest), GROUP), rest])

    held_tokens, terms, side = lax.cond(
        lax.axis_index("core") == 0, in_one, in_two, tokens[0], cotangent[0], momentum[0], weight, kept
    )
    sent, change, held, held_tokens = raise_and_pick(terms, side, held_tokens, table, sites, rows_all, nx)

    fresh = update(exchange(sent, SITE), held, table, nz * nyh)
    mine = lax.cond(
        lax.axis_index("core") == 0,
        lambda value: exchange(value, ("z", "yh")),
        lambda value: exchange(value, ("yh", "z")),
        fresh,
    )
    other = lax.ppermute(mine, "core", [(0, 1), (1, 0)])
    scores, moment_new = finish(exchange(project(held_tokens, mine, other, change), GROUP), momentum[0], tok)
    return (scores[None], moment_new[None])


def solution(mesh):
    grid = Mesh(mesh.devices.reshape(8, 2, 4, 2, 4), ("z", "core", "yh", "yl", "x"))
    placed = (
        P(SITE, DEV, None),
        P(SITE, DEV, None),
        P(DEV, None),
        P(SITE, DEV, None),
        P(None, DEV, None, None),
    )
    return jax.shard_map(
        shards,
        mesh=grid,
        in_specs=placed,
        out_specs=(P(SITE, DEV, None), P(SITE, DEV, None)),
        check_vma=False,
    )
```
